32 devices in a mesh: grp: 2 (over y), tile: 8 (over z, x), ch: 2 (over core).
Axes of the slice: x: 2, y: 2, z: 4, core: 2. Of those that a mesh axis runs over, the one named last changes fastest.
Arguments:
- source: bfloat16 [64, 131072], P('ch', ('grp', 'tile')), parts along dimension 1, may hold values from -6 to 6
- request_rows: int32 [8, 8, 2048], P('tile'), may hold values from 0 to 8191, as said below
- cell_slots: int32 [8, 4, 4096], P('tile'), may hold values from 0 to 16383, as said below
- cell_counts: int32 [8, 4, 4096], P('tile'), may hold values from 1 to 16
- seam: int32 [8, 4], replicated, may hold values from 0 to 7
- conv_first: bfloat16 [3, 3, 128, 64], P(None, None, 'ch'), may hold values from -0.25 to 0.25
- bias_first: float32 [128], P('ch'), may hold values from -3 to 3
- conv_second: bfloat16 [3, 3, 64, 128], replicated, may hold values from -0.1875 to 0.1875
- bias_second: float32 [64], replicated, may hold values from -3 to 3
Outputs:
- forecast: bfloat16 [16, 64, 4096], P(('grp', 'tile'), 'ch'), parts along dimension 0
The draws below stay inside these ranges and needn't reach their ends.
There are 2 independent parts, one for each index of `grp`. The reference program is written for one: setup_inputs(seed, part) draws one part's arguments, and reference() takes and returns one part's arrays. A program takes and returns all parts, laid end to end along the dimension named above; an argument that names none is the same for every part. Nothing has to cross between parts.
Inputs may be any that keep to these rules, and one draw needn't show every extreme that they name: request_rows[t, s, j] is a row among the 8192 source cells held at tile index s. cell_slots[t, k, p] names the column s * 2048 + j of fetched[t].
All inputs are finite; a program needn't handle non-finite values.
Results may differ from the reference program's by a relative error of at most 0.0047.
Values may be sent and summed in bfloat16 or wider, within the bound.
A program may use at most 64 MiB of HBM per device.

```python
import math
import jax
import jax.numpy as jnp
from jax import lax

CIN = 64
HID = 128
SIDE = 64
TILE_ROW = 4
ENTRIES = 4
SRC_DEV = 8192
TILES = 8
CAP = 2048
CELLS = 4096
SRC = 65536


def busiest_owner(key):
    offset_draw = jax.random.randint(jax.random.fold_in(key, 12), (), 0, TILES)
    return (jnp.arange(TILES, dtype=jnp.int32) + offset_draw) % TILES


def live_counts(key):
    raw_draw = jax.random.randint(jax.random.fold_in(key, 11), (TILES, TILES), 0, CAP)
    counts = CAP - raw_draw * raw_draw // CAP
    busiest = busiest_owner(key)
    marked = jnp.arange(TILES, dtype=jnp.int32)[None, :] == busiest[:, None]
    return jnp.where(marked, CAP, counts).astype(jnp.int32)


def draw_request_rows(key, part):
    live_table = live_counts(key)
    key = jax.random.fold_in(key, 3)
    row_draw = jax.random.randint(key, (TILES, TILES, CAP), 0, SRC_DEV)
    slot_index = jnp.arange(CAP, dtype=jnp.int32)
    return jnp.where(slot_index[None, None, :] < live_table[:, :, None], row_draw, 0).astype(jnp.int32)


def draw_cell_slots(key, part):
    live_table = live_counts(key)
    busiest = busiest_owner(key)
    key = jax.random.fold_in(key, 5)
    owner_draw = jax.random.randint(jax.random.fold_in(key, 1), (TILES, ENTRIES, CELLS), 0, TILES)
    pick_draw = jax.random.randint(jax.random.fold_in(key, 2), (TILES, ENTRIES, CELLS), 0, CAP)
    live_limit = jnp.take_along_axis(live_table, owner_draw.reshape(TILES, ENTRIES * CELLS), axis=1).reshape(TILES, ENTRIES, CELLS)
    slot_draw = owner_draw * CAP + pick_draw % live_limit
    forced = busiest * CAP + CAP - 1
    return slot_draw.at[:, 0, 0].set(forced).astype(jnp.int32)


def plant(drawn, rng, low, high):
    place = [jax.random.randint(jax.random.fold_in(rng, axis), (), 0, length) for axis, length in enumerate(drawn.shape)]
    widest = drawn.shape.index(max(drawn.shape))
    beside = place[:widest] + [(place[widest] + 1) % drawn.shape[widest]] + place[widest + 1:]
    return drawn.at[tuple(place)].set(low).at[tuple(beside)].set(high)


def shard_levels(rng, extent, cuts, least, top_value):
    def one(position, blocks):
        heights = jax.random.uniform(jax.random.fold_in(jax.random.fold_in(rng, 6), position), (blocks,), jnp.float32, least / len(cuts), top_value / len(cuts))
        return jnp.repeat(jnp.exp(heights), extent[position] // blocks).reshape((-1,) + (1,) * (len(extent) - position - 1))

    level = one(*cuts[0])
    for cut in cuts[1:]:
        level = level * one(*cut)
    return level


def centred(key, shape, spread, bound, cuts=(), kind=jnp.bfloat16):
    level = shard_levels(key, shape, cuts, -0.22, 0.18) if cuts else 1.0
    drawn = jax.random.normal(key, shape, jnp.float32) * spread * level
    return jnp.minimum(jnp.maximum(drawn, -bound), bound).astype(kind)


def setup_inputs(seed: int = 0, part: int = 0) -> dict:
    seeds = jax.random.split(jax.random.key(seed), 10)
    part_splits = jax.random.split(jax.random.fold_in(seeds[9], part), 10)
    return {
        "source": centred(part_splits[0], (CIN, SRC), 1.0, 6.0, ((0, 2), (1, 8))),
        "request_rows": draw_request_rows(jax.random.fold_in(seeds[9], 71), part),
        "cell_slots": draw_cell_slots(jax.random.fold_in(seeds[9], 71), part),
        "cell_counts": plant(jax.random.randint(seeds[3], (TILES, ENTRIES, CELLS), 1, 17), jax.random.fold_in(seeds[3], 1), 1, 16).astype(jnp.int32),
        "seam": plant(jax.random.randint(seeds[4], (TILES, 4), 0, 8), jax.random.fold_in(seeds[4], 1), 0, 7).astype(jnp.int32),
        "conv_first": centred(seeds[5], (3, 3, HID, CIN), (9 * CIN) ** -0.5, 0.25, ((2, 2),)),
        "bias_first": centred(seeds[6], (HID,), 0.5, 3.0, ((0, 2),), jnp.float32),
        "conv_second": centred(seeds[7], (3, 3, CIN, HID), (9 * HID) ** -0.5, 0.1875),
        "bias_second": centred(seeds[8], (CIN,), 0.5, 3.0, (), jnp.float32),
    }


def seam_moves():
    return ((0, TILE_ROW), (1, -1), (2, -TILE_ROW), (3, 1))


def remap_cells(fetched, slot_table, counts):
    weights = counts.astype(jnp.float32)
    count_total = weights[0]
    for entry in range(1, slot_table.shape[0]):
        count_total = count_total + weights[entry]
    weighted = None
    for entry in range(slot_table.shape[0]):
        picked = jnp.take(fetched, slot_table[entry], axis=1).astype(jnp.float32)
        contribution = weights[entry][None, :] * picked
        weighted = contribution if weighted is None else weighted + contribution
    return (weighted / count_total[None, :]).astype(jnp.bfloat16)


def orient(rim_edges, seam_code):
    chosen = lax.dynamic_index_in_dim(rim_edges, seam_code % 4, 0, keepdims=False)
    return jnp.where(seam_code >= 4, chosen[:, ::-1], chosen)


def assemble(field_grid, north_rim, east_rim, south_rim, west_rim):
    def corner(first_rim, second_rim):
        return ((first_rim.astype(jnp.float32) + second_rim.astype(jnp.float32)) * 0.5).astype(jnp.bfloat16)[:, None]

    top_row = jnp.concatenate([corner(north_rim[:, 0], west_rim[:, 0]), north_rim, corner(north_rim[:, -1], east_rim[:, 0])], axis=1)
    bottom_row = jnp.concatenate([corner(south_rim[:, 0], west_rim[:, -1]), south_rim, corner(south_rim[:, -1], east_rim[:, -1])], axis=1)
    middle = jnp.concatenate([west_rim[:, :, None], field_grid, east_rim[:, :, None]], axis=2)
    return jnp.concatenate([top_row[:, None], middle, bottom_row[:, None]], axis=1)


def flatten_weights(weights):
    return jnp.transpose(weights, (2, 0, 1, 3)).reshape(weights.shape[2], 9 * weights.shape[3])


def convolve(padded, weight_matrix):
    channels = padded.shape[0]
    side_len = padded.shape[1] - 2
    block_rows = math.gcd(side_len, 16)

    def conv_block(row_start):
        row_slab = lax.dynamic_slice_in_dim(padded, row_start, block_rows + 2, 1)
        windows = [row_slab[:, vertical:vertical + block_rows, lateral:lateral + side_len] for vertical in range(3) for lateral in range(3)]
        patches = jnp.stack(windows).reshape(9 * channels, block_rows * side_len)
        return jnp.dot(weight_matrix, patches, preferred_element_type=jnp.float32)

    starts = jnp.arange(side_len // block_rows, dtype=jnp.int32) * block_rows
    blocks = lax.map(conv_block, starts)
    return jnp.transpose(blocks, (1, 0, 2)).reshape(weight_matrix.shape[0], side_len * side_len)


def rim_stack(fields):
    return jnp.stack([fields[:, :, 0, :], fields[:, :, :, -1], fields[:, :, -1, :], fields[:, :, :, 0]], axis=1)


def seam_rims(all_edges, seam, tile_id):
    vectors = []
    for direction, step_by in seam_moves():
        neighbour = (tile_id - step_by) % TILES
        vectors.append(orient(all_edges[neighbour], seam[tile_id, direction]))
    return vectors


def reference(source, request_rows, cell_slots, cell_counts, seam, conv_first, bias_first, conv_second, bias_second):
    owners = jnp.arange(TILES, dtype=jnp.int32)[:, None] * SRC_DEV

    def remap_tile(pieces):
        wanted, slot_table, counts = pieces
        fetched = jnp.take(source, (owners + wanted).reshape(-1), axis=1)
        return remap_cells(fetched, slot_table, counts)

    remapped = lax.map(remap_tile, (request_rows, cell_slots, cell_counts))
    tile_grids = remapped.reshape(TILES, CIN, SIDE, SIDE)
    first_edges = rim_stack(tile_grids)
    first_matrix = flatten_weights(conv_first)
    tile_ids = jnp.arange(TILES, dtype=jnp.int32)

    def first_layer(tile_id):
        padded = assemble(tile_grids[tile_id], *seam_rims(first_edges, seam, tile_id))
        activated = jax.nn.gelu(convolve(padded, first_matrix) + bias_first[:, None], approximate=True)
        return activated.astype(jnp.bfloat16).reshape(HID, SIDE, SIDE)

    hidden = lax.map(first_layer, tile_ids)
    second_edges = rim_stack(hidden)
    second_matrix = flatten_weights(conv_second)

    def second_layer(tile_id):
        padded = assemble(hidden[tile_id], *seam_rims(second_edges, seam, tile_id))
        response = convolve(padded, second_matrix) + bias_second[:, None]
        return (remapped[tile_id].astype(jnp.float32) + response).astype(jnp.bfloat16)

    return lax.map(second_layer, tile_ids)
```

```python
import functools

import jax
import jax.numpy as jnp
from jax import lax
from jax.experimental import pallas as pl
from jax.experimental.pallas import tpu as pltpu
from jax.sharding import PartitionSpec as P

SIDE = 64
TILE_ROW = 4
LANES = 128
MOVES = (TILE_ROW, -1, -TILE_ROW, 1)
BF = jnp.bfloat16
F32 = jnp.float32
SMEM = pl.BlockSpec(memory_space=pltpu.SMEM)
VMEM = pl.BlockSpec(memory_space=pltpu.VMEM)


def swap_core(x):
    return lax.ppermute(x, "ch", [(0, 1), (1, 0)])


def from_behind(x, by):
    size = lax.axis_size("tile")
    return lax.ppermute(x, "tile", [(i, (i + by) % size) for i in range(size)])


def pick_kernel(chunk, first_ref, second_ref, table_ref, out_ref, rows_ref):
    low = lax.broadcasted_iota(jnp.int32, (1, LANES), 1) < SIDE
    total = out_ref.shape[0]

    def step(block, carry):
        base = block * chunk

        def group(g, inner):
            for u in range(8):
                at = g * 8 + u
                left = table_ref[pl.ds(first_ref[base + at], 1), :]
                right = table_ref[pl.ds(second_ref[base + at], 1), :]
                rows_ref[pl.ds(at, 1), :] = jnp.where(low, left, right)
            return inner

        lax.fori_loop(0, chunk // 8, group, 0)
        out_ref[pl.ds(pl.multiple_of(base, chunk), chunk), :] = rows_ref[...].astype(BF)
        return carry

    lax.fori_loop(0, total // chunk, step, 0)


def pick_rows(first, second, table):
    total = first.shape[0]
    chunk = 128
    return pl.pallas_call(
        functools.partial(pick_kernel, chunk),
        out_shape=jax.ShapeDtypeStruct((total, LANES), BF),
        in_specs=[SMEM, SMEM, VMEM],
        out_specs=VMEM,
        scratch_shapes=[pltpu.VMEM((chunk, LANES), F32)],
        compiler_params=pltpu.CompilerParams(vmem_limit_bytes=32 * 2**20),
        name="pick_rows",
    )(first, second, table)


def remap_kernel(chunk, slots_ref, counts_ref, low_ref, high_ref, out_ref, table_ref, rows_ref):
    part = low_ref.shape[0]

    def fill(block, carry):
        at = pl.multiple_of(block * 128, 128)
        for which, ref in enumerate((low_ref, high_ref)):
            piece = ref[pl.ds(at, 128), :].astype(F32)
            table_ref[pl.ds(which * part + at, 128), :] = piece
            table_ref[pl.ds((2 + which) * part + at, 128), :] = pltpu.roll(piece, SIDE, 1)
        return carry

    lax.fori_loop(0, part // 128, fill, 0)
    entries = slots_ref.shape[0]
    cells = out_ref.shape[0]

    def step(block, carry):
        base = block * chunk

        def group(g, inner):
            for u in range(8):
                at = g * 8 + u
                for k in range(entries):
                    rows_ref[k, pl.ds(at, 1), :] = table_ref[pl.ds(slots_ref[k, base + at], 1), :]
            return inner

        lax.fori_loop(0, chunk // 8, group, 0)
        here = pl.ds(pl.multiple_of(base, chunk), chunk)
        weights = counts_ref[here, :]
        count = weights[:, 0:1]
        summed = weights[:, 0:1] * rows_ref[0]
        for k in range(1, entries):
            count = count + weights[:, k : k + 1]
            summed = summed + weights[:, k : k + 1] * rows_ref[k]
        out_ref[here, :] = (summed / count)[:, :SIDE].astype(BF)
        return carry

    lax.fori_loop(0, cells // chunk, step, 0)


def remap_cells(slots, counts, low, high):
    entries, cells = slots.shape
    chunk = 128
    return pl.pallas_call(
        functools.partial(remap_kernel, chunk),
        out_shape=jax.ShapeDtypeStruct((cells, SIDE), BF),
        in_specs=[SMEM, VMEM, VMEM, VMEM],
        out_specs=VMEM,
        scratch_shapes=[
            pltpu.VMEM((4 * low.shape[0], LANES), F32),
            pltpu.VMEM((entries, chunk, LANES), F32),
        ],
        compiler_params=pltpu.CompilerParams(vmem_limit_bytes=40 * 2**20),
        name="remap_cells",
    )(slots, counts, low, high)


def seam_choice(seam, position):
    tiles = seam.shape[0]
    place = jnp.arange(SIDE, dtype=jnp.int32)
    rows = []
    for side, by in enumerate(MOVES):
        code = lax.dynamic_index_in_dim(seam, (position + by) % tiles, 0, keepdims=False)[side]
        rows.append((code % 4) * SIDE + jnp.where(code >= 4, SIDE - 1 - place, place))
    wanted = jnp.concatenate(rows)
    return (wanted[:, None] == jnp.arange(4 * SIDE, dtype=jnp.int32)[None, :]).astype(BF)


def extend_half(half, choice, core):
    height = half.shape[0]
    pack = jnp.concatenate([half[0], half[-1], half[:, 0], half[:, -1]])
    other = swap_core(pack)
    upper = jnp.where(core == 0, pack, other)
    lower = jnp.where(core == 0, other, pack)
    a, b = 2 * SIDE, 2 * SIDE + height
    edges = jnp.concatenate([upper[:SIDE], upper[b:], lower[b:], lower[SIDE:a], upper[a:b], lower[a:b]])
    chosen = jnp.dot(choice, edges, preferred_element_type=F32).astype(BF)
    north, east, south, west = [
        from_behind(chosen[d * SIDE : (d + 1) * SIDE], by) for d, by in enumerate(MOVES)
    ]

    def corner(one, two):
        return ((one.astype(F32) + two.astype(F32)) * 0.5).astype(BF)[None]

    is_upper = core == 0
    above = jnp.where(is_upper, north, upper[SIDE:a])
    below = jnp.where(is_upper, lower[:SIDE], south)

    def column(rim, place):
        first = jnp.concatenate([corner(north[place], rim[0]), rim[: height + 1]])
        second = jnp.concatenate([rim[height - 1 :], corner(south[place], rim[-1])])
        return jnp.where(is_upper, first, second)[:, None]

    middle = jnp.concatenate([above[None], half, below[None]])
    return jnp.concatenate([column(west, 0), middle, column(east, SIDE - 1)], axis=1)


def convolve(padded, kernel):
    return lax.conv_general_dilated(
        padded[None],
        kernel,
        (1, 1),
        "VALID",
        dimension_numbers=("NHWC", "HWIO", "NHWC"),
        preferred_element_type=F32,
    )[0]


def shards(source, request_rows, cell_slots, cell_counts, seam, conv_first, bias_first, conv_second, bias_second):
    position = lax.axis_index("tile")
    core = lax.axis_index("ch")
    tiles, slots_each = request_rows.shape[1], request_rows.shape[2]
    share = slots_each // 2
    quarter = share // 2
    cells_half = cell_slots.shape[2] // 2

    requests = lax.dynamic_slice_in_dim(request_rows[0], core * share, share, 1)
    wanted = lax.all_to_all(requests, "tile", split_axis=0, concat_axis=0, tiled=True)
    sibling = swap_core(source)
    rows = jnp.where(
        core == 0, jnp.concatenate([source, sibling]), jnp.concatenate([sibling, source])
    ).T.astype(F32)
    table = jnp.concatenate([rows, rows], axis=1)
    wanted = wanted.reshape(tiles, 2, quarter)
    picked = pick_rows(wanted[:, 0].reshape(-1), wanted[:, 1].reshape(-1), table)
    arrived = lax.all_to_all(
        picked.reshape(tiles, quarter, LANES), "tile", split_axis=0, concat_axis=0, tiled=True
    ).reshape(tiles * quarter, LANES)
    across = swap_core(arrived)
    low = jnp.where(core == 0, arrived, across)
    high = jnp.where(core == 0, across, arrived)

    slots = lax.dynamic_slice_in_dim(cell_slots[0], core * cells_half, cells_half, 1)
    counts = lax.dynamic_slice_in_dim(cell_counts[0], core * cells_half, cells_half, 1)
    owner, place = slots // slots_each, slots % slots_each
    served, inside = place // share, place % share
    part = tiles * quarter
    table_rows = (inside // quarter) * (2 * part) + served * part + owner * quarter + inside % quarter
    remapped = remap_cells(table_rows, counts.astype(F32).T, low, high)

    choice = seam_choice(seam, position)
    first_kernel = jnp.transpose(lax.all_gather(conv_first, "ch", axis=2, tiled=True), (0, 1, 3, 2))
    first_bias = lax.all_gather(bias_first, "ch", axis=0, tiled=True)
    height = cells_half // SIDE
    grid = remapped.reshape(height, SIDE, SIDE)
    activated = jax.nn.gelu(convolve(extend_half(grid, choice, core), first_kernel) + first_bias, approximate=True)
    hidden = activated.astype(BF)
    second_kernel = jnp.transpose(conv_second, (0, 1, 3, 2))
    response = convolve(extend_half(hidden, choice, core), second_kernel) + bias_second
    result = (grid.astype(F32) + response).astype(BF).reshape(cells_half, SIDE).T
    mine = SIDE // 2
    kept = lax.dynamic_slice_in_dim(result, core * mine, mine, 0)
    sent = swap_core(lax.dynamic_slice_in_dim(result, (1 - core) * mine, mine, 0))
    return jnp.where(
        core == 0, jnp.concatenate([kept, sent], axis=1), jnp.concatenate([sent, kept], axis=1)
    )[None]


def solution(mesh):
    in_specs = (
        P("ch", ("grp", "tile")),
        P("tile", None, None),
        P("tile", None, None),
        P("tile", None, None),
        P(),
        P(None, None, "ch", None),
        P("ch"),
        P(),
        P(),
    )
    out_specs = P(("grp", "tile"), "ch", None)
    return jax.shard_map(shards, mesh=mesh, in_specs=in_specs, out_specs=out_specs, check_vma=False)
```

```python
import functools

import jax
import jax.numpy as jnp
from jax import lax
from jax.experimental import pallas as pl
from jax.experimental.pallas import tpu as pltpu
from jax.sharding import PartitionSpec as P

SIDE = 64
TILE_ROW = 4
LANES = 128
MOVES = (TILE_ROW, -1, -TILE_ROW, 1)
BF = jnp.bfloat16
F32 = jnp.float32
SMEM = pl.BlockSpec(memory_space=pltpu.SMEM)
VMEM = pl.BlockSpec(memory_space=pltpu.VMEM)


def swap_core(x):
    return lax.ppermute(x, "ch", [(0, 1), (1, 0)])


def from_behind(x, by):
    size = lax.axis_size("tile")
    return lax.ppermute(x, "tile", [(i, (i + by) % size) for i in range(size)])


def pick_kernel(chunk, first_ref, second_ref, table_ref, out_ref, rows_ref):
    low = lax.broadcasted_iota(jnp.int32, (1, LANES), 1) < SIDE
    total = out_ref.shape[0]

    def step(block, carry):
        base = block * chunk

        def group(g, inner):
            for u in range(8):
                at = g * 8 + u
                left = table_ref[pl.ds(first_ref[base + at], 1), :]
                right = table_ref[pl.ds(second_ref[base + at], 1), :]
                rows_ref[pl.ds(at, 1), :] = jnp.where(low, left, right)
            return inner

        lax.fori_loop(0, chunk // 8, group, 0)
        out_ref[pl.ds(pl.multiple_of(base, chunk), chunk), :] = rows_ref[...].astype(BF)
        return carry

    lax.fori_loop(0, total // chunk, step, 0)


def pick_rows(first, second, table):
    total = first.shape[0]
    chunk = 128
    return pl.pallas_call(
        functools.partial(pick_kernel, chunk),
        out_shape=jax.ShapeDtypeStruct((total, LANES), BF),
        in_specs=[SMEM, SMEM, VMEM],
        out_specs=VMEM,
        scratch_shapes=[pltpu.VMEM((chunk, LANES), F32)],
        compiler_params=pltpu.CompilerParams(vmem_limit_bytes=32 * 2**20),
        name="pick_rows",
    )(first, second, table)


def remap_kernel(chunk, slots_ref, counts_ref, low_ref, high_ref, out_ref, table_ref, rows_ref):
    part = low_ref.shape[0]

    def fill(block, carry):
        at = pl.multiple_of(block * 128, 128)
        for which, ref in enumerate((low_ref, high_ref)):
            piece = ref[pl.ds(at, 128), :].astype(F32)
            table_ref[pl.ds(which * part + at, 128), :] = piece
            table_ref[pl.ds((2 + which) * part + at, 128), :] = pltpu.roll(piece, SIDE, 1)
        return carry

    lax.fori_loop(0, part // 128, fill, 0)
    entries = slots_ref.shape[0]
    cells = out_ref.shape[0]

    def step(block, carry):
        base = block * chunk

        def group(g, inner):
            for u in range(8):
                at = g * 8 + u
                for k in range(entries):
                    rows_ref[k, pl.ds(at, 1), :] = table_ref[pl.ds(slots_ref[k, base + at], 1), :]
            return inner

        lax.fori_loop(0, chunk // 8, group, 0)
        here = pl.ds(pl.multiple_of(base, chunk), chunk)
        weights = counts_ref[here, :]
        count = weights[:, 0:1]
        summed = weights[:, 0:1] * rows_ref[0]
        for k in range(1, entries):
            count = count + weights[:, k : k + 1]
            summed = summed + weights[:, k : k + 1] * rows_ref[k]
        out_ref[here, :] = (summed / count)[:, :SIDE].astype(BF)
        return carry

    lax.fori_loop(0, cells // chunk, step, 0)


def remap_cells(slots, counts, low, high):
    entries, cells = slots.shape
    chunk = 128
    return pl.pallas_call(
        functools.partial(remap_kernel, chunk),
        out_shape=jax.ShapeDtypeStruct((cells, SIDE), BF),
        in_specs=[SMEM, VMEM, VMEM, VMEM],
        out_specs=VMEM,
        scratch_shapes=[
            pltpu.VMEM((4 * low.shape[0], LANES), F32),
            pltpu.VMEM((entries, chunk, LANES), F32),
        ],
        compiler_params=pltpu.CompilerParams(vmem_limit_bytes=40 * 2**20),
        name="remap_cells",
    )(slots, counts, low, high)


def seam_choice(seam, position, core, height):
    tiles = seam.shape[0]
    place = jnp.arange(SIDE, dtype=jnp.int32)
    rows = []
    for side, by in enumerate(MOVES):
        code = lax.dynamic_index_in_dim(seam, (position + by) % tiles, 0, keepdims=False)[side]
        edge = code % 4
        cell = jnp.where(code >= 4, SIDE - 1 - place, place)
        near = cell - core * height
        column = jnp.where((near >= 0) & (near < height), 2 * SIDE + jnp.where(edge == 1, height, 0) + near, -1)
        row = jnp.where(core == edge // 2, core * SIDE + cell, -1)
        rows.append(jnp.where(edge % 2 == 0, row, column))
    wanted = jnp.concatenate(rows)
    width = 2 * SIDE + 2 * height
    return (wanted[:, None] == jnp.arange(width, dtype=jnp.int32)[None, :]).astype(BF)


def block_kernel(
    half_ref, choice_ref, first_ref, first_bias_ref, second_ref, second_bias_ref, out_ref,
    field, hidden, west_buf, east_buf, left_shift, right_shift, mid_buf, pack_one, pack_two,
    send_one, send_two, recv_one, recv_two, halo_one, halo_two, other_first, other_bias,
    first_full, turned, send_sems, recv_sems, side_sems,
):
    grp, tile, core = (lax.axis_index(name) for name in ("grp", "tile", "ch"))
    tiles = lax.axis_size("tile")
    sibling = (grp, tile, 1 - core)
    upper = core == 0
    cells = half_ref.shape[0]
    height = cells // SIDE
    rows = cells + 2 * SIDE
    start = 8
    body = start + SIDE
    targets = [lax.rem(tile + by + tiles, tiles) for by in MOVES]
    sources = [lax.rem(tile - by + tiles, tiles) for by in MOVES]

    barrier = pltpu.get_barrier_semaphore()
    pl.semaphore_signal(barrier, inc=1, device_id=sibling, device_id_type=pl.DeviceIdType.MESH)
    for other in targets:
        for c in range(2):
            pl.semaphore_signal(barrier, inc=1, device_id=(grp, other, c), device_id_type=pl.DeviceIdType.MESH)

    field[pl.ds(body, cells), :] = half_ref[...].astype(F32)
    pl.semaphore_wait(barrier, 9)

    def remote(src, dst, send_sem, recv_sem, device):
        return pltpu.make_async_remote_copy(
            src_ref=src, dst_ref=dst, send_sem=send_sem, recv_sem=recv_sem,
            device_id=device, device_id_type=pl.DeviceIdType.MESH,
        )

    def begin(rnd, grid, pack, send, recv, halo):
        pack[0:SIDE, :] = grid[body : body + SIDE, :].astype(BF)
        pack[SIDE : 2 * SIDE, :] = grid[body + cells - SIDE : body + cells, :].astype(BF)
        a = 2 * SIDE
        pack[a : a + height, :] = grid[pl.ds(body, height, stride=SIDE), :].astype(BF)
        pack[a + height : a + 2 * height, :] = grid[pl.ds(body + SIDE - 1, height, stride=SIDE), :].astype(BF)
        rims = jnp.dot(choice_ref[...], pack[...], preferred_element_type=F32).astype(BF)
        for d in range(4):
            send[d] = rims[d * SIDE : (d + 1) * SIDE]
        copies = []
        for d in range(4):
            for c in range(2):
                copies.append(
                    remote(
                        send.at[d], recv.at[core, d], send_sems.at[rnd, 2 * d + c],
                        recv_sems.at[rnd, core * 4 + d], (grp, targets[d], c),
                    )
                )
        inner = pl.multiple_of((1 - core) * SIDE, SIDE)
        copies.append(
            remote(pack.at[pl.ds(inner, SIDE), :], halo, send_sems.at[rnd, 8], recv_sems.at[rnd, 8], sibling)
        )
        for copy in copies:
            copy.start()
        return copies

    def finish(rnd, copies, grid, send, recv, halo, left, right, mid, width):
        lanes = slice(0, width)
        for d in range(4):
            for c in range(2):
                remote(
                    send.at[d], recv.at[c, d], send_sems.at[rnd, 2 * d + c],
                    recv_sems.at[rnd, c * 4 + d], (grp, sources[d], c),
                ).wait_recv()
        copies[-1].wait_recv()
        north, east, south, west = [recv[0, d].astype(F32) + recv[1, d].astype(F32) for d in range(4)]
        inside = halo[...].astype(F32)
        grid[start:body, :] = jnp.where(upper, north, inside)
        grid[body + cells : body + cells + SIDE, :] = jnp.where(upper, inside, south)

        def corner(one, two):
            return ((one + two) * 0.5).astype(BF).astype(F32)

        def column(buf, rim, place):
            buf[8 : 8 + SIDE, lanes] = rim
            buf[7:8, lanes] = corner(north[place : place + 1], rim[0:1])
            buf[8 + SIDE : 9 + SIDE, lanes] = corner(south[place : place + 1], rim[SIDE - 1 : SIDE])
            return jnp.where(
                upper, buf[7 : 9 + height, lanes], buf[7 + SIDE - height : 9 + SIDE, lanes]
            )

        west_cells = column(west_buf, west, 0)
        east_cells = column(east_buf, east, SIDE - 1)
        left[...] = grid[start - 1 : start - 1 + rows, :]
        left[pl.ds(0, height + 2, stride=SIDE), :] = west_cells
        right[...] = grid[start + 1 : start + 1 + rows, :]
        right[pl.ds(SIDE - 1, height + 2, stride=SIDE), :] = east_cells
        mid[0, :, lanes] = left[...].astype(BF)
        mid[1, :, lanes] = grid[start : start + rows, :].astype(BF)
        mid[2, :, lanes] = right[...].astype(BF)
        for copy in copies:
            copy.wait_send()

    block = 256

    def convolve(mid, weights, at, width):
        total = None
        for a in range(3):
            for b in range(3):
                piece = mid[b, pl.ds(pl.multiple_of(at + a * SIDE, SIDE), block), 0:width]
                term = jnp.dot(piece, weights[3 * a + b], preferred_element_type=F32)
                total = term if total is None else total + term
        return total

    weight_copy = remote(first_ref, other_first, side_sems.at[0], side_sems.at[1], sibling)
    bias_copy = remote(first_bias_ref, other_bias, side_sems.at[2], side_sems.at[3], sibling)
    copies = begin(0, field, pack_one, send_one, recv_one, halo_one)
    weight_copy.start()
    bias_copy.start()
    weight_copy.wait()
    bias_copy.wait()
    mine, other = first_ref[...], other_first[...]
    first_full[:, :, 0:SIDE] = jnp.where(upper, mine, other)
    first_full[:, :, SIDE:] = jnp.where(upper, other, mine)
    mine, other = first_bias_ref[0:1, :], other_bias[0:1, :]
    bias = jnp.concatenate([jnp.where(upper, mine, other), jnp.where(upper, other, mine)], axis=1)
    finish(0, copies, field, send_one, recv_one, halo_one, left_shift[0], right_shift[0], mid_buf, SIDE)

    def first(step, carry):
        at = pl.multiple_of(step * block, block)
        v = convolve(mid_buf, first_full, at, SIDE) + bias
        act = 0.5 * v * (1.0 + jnp.tanh(0.7978845608028654 * (v + 0.044715 * (v * v * v))))
        hidden[pl.ds(pl.multiple_of(body + at, 8), block), :] = act.astype(BF).astype(F32)
        return carry

    lax.fori_loop(0, cells // block, first, 0)
    copies = begin(1, hidden, pack_two, send_two, recv_two, halo_two)
    finish(1, copies, hidden, send_two, recv_two, halo_two, left_shift[1], right_shift[1], mid_buf, 2 * SIDE)

    def second(step, carry):
        at = pl.multiple_of(step * block, block)
        v = convolve(mid_buf, second_ref, at, 2 * SIDE) + second_bias_ref[...]
        v = v + field[pl.ds(pl.multiple_of(body + at, 8), block), :]
        turned[:, pl.ds(at, block)] = v.T.astype(BF)
        return carry

    lax.fori_loop(0, cells // block, second, 0)
    share = SIDE // 2
    away = remote(
        turned.at[pl.ds(pl.multiple_of((1 - core) * share, share), share), :],
        out_ref.at[:, pl.ds(pl.multiple_of(core * cells, cells), cells)],
        side_sems.at[4], side_sems.at[5], sibling,
    )
    away.start()
    out_ref[:, pl.ds(pl.multiple_of(core * cells, cells), cells)] = turned[
        pl.ds(pl.multiple_of(core * share, share), share), :
    ]
    away.wait()


def conv_block(half, choice, first, first_bias, second, second_bias):
    cells, chans = half.shape
    hid = 2 * chans
    rows = cells + 2 * SIDE
    pack = choice.shape[1]
    shape = pltpu.VMEM

    def kernel(*refs):
        ins, rest = refs[:7], list(refs[7:])
        l1, l2, r1, r2 = rest[4:8]
        block_kernel(*ins, *rest[:4], (l1, l2), (r1, r2), *rest[8:])

    return pl.pallas_call(
        kernel,
        out_shape=jax.ShapeDtypeStruct((chans // 2, 2 * cells), BF),
        in_specs=[VMEM] * 6,
        out_specs=VMEM,
        scratch_shapes=[
            shape((rows + 16, chans), F32), shape((rows + 16, hid), F32),
            shape((SIDE + 16, hid), F32), shape((SIDE + 16, hid), F32),
            shape((rows, chans), F32), shape((rows, hid), F32),
            shape((rows, chans), F32), shape((rows, hid), F32),
            shape((3, rows, hid), BF),
            shape((pack, chans), BF), shape((pack, hid), BF),
            shape((4, SIDE, chans), BF), shape((4, SIDE, hid), BF),
            shape((2, 4, SIDE, chans), BF), shape((2, 4, SIDE, hid), BF),
            shape((SIDE, chans), BF), shape((SIDE, hid), BF),
            shape(first.shape, BF), shape(first_bias.shape, F32),
            shape((9, chans, hid), BF), shape((chans, cells), BF),
            pltpu.SemaphoreType.DMA((2, 9)), pltpu.SemaphoreType.DMA((2, 9)), pltpu.SemaphoreType.DMA((6,)),
        ],
        compiler_params=pltpu.CompilerParams(
            collective_id=0, has_side_effects=True, vmem_limit_bytes=48 * 2**20
        ),
        name="conv_block",
    )(half, choice, first, first_bias, second, second_bias)


def shards(source, request_rows, cell_slots, cell_counts, seam, conv_first, bias_first, conv_second, bias_second):
    position = lax.axis_index("tile")
    core = lax.axis_index("ch")
    tiles, slots_each = request_rows.shape[1], request_rows.shape[2]
    share = slots_each // 2
    quarter = share // 2
    cells_half = cell_slots.shape[2] // 2

    requests = lax.dynamic_slice_in_dim(request_rows[0], core * share, share, 1)
    wanted = lax.all_to_all(requests, "tile", split_axis=0, concat_axis=0, tiled=True)
    sibling = swap_core(source)
    rows = jnp.where(
        core == 0, jnp.concatenate([source, sibling]), jnp.concatenate([sibling, source])
    ).T.astype(F32)
    table = jnp.concatenate([rows, rows], axis=1)
    wanted = wanted.reshape(tiles, 2, quarter)
    picked = pick_rows(wanted[:, 0].reshape(-1), wanted[:, 1].reshape(-1), table)
    arrived = lax.all_to_all(
        picked.reshape(tiles, quarter, LANES), "tile", split_axis=0, concat_axis=0, tiled=True
    ).reshape(tiles * quarter, LANES)
    across = swap_core(arrived)
    low = jnp.where(core == 0, arrived, across)
    high = jnp.where(core == 0, across, arrived)

    slots = lax.dynamic_slice_in_dim(cell_slots[0], core * cells_half, cells_half, 1)
    counts = lax.dynamic_slice_in_dim(cell_counts[0], core * cells_half, cells_half, 1)
    owner, place = slots // slots_each, slots % slots_each
    served, inside = place // share, place % share
    part = tiles * quarter
    table_rows = (inside // quarter) * (2 * part) + served * part + owner * quarter + inside % quarter
    remapped = remap_cells(table_rows, counts.astype(F32).T, low, high)

    choice = seam_choice(seam, position, core, cells_half // SIDE)

    def arrange(weights):
        return jnp.transpose(weights, (0, 1, 3, 2)).reshape(9, weights.shape[3], weights.shape[2])

    bias_rows = jnp.broadcast_to(bias_first[None], (8, bias_first.shape[0]))
    return conv_block(
        remapped, choice, arrange(conv_first), bias_rows, arrange(conv_second), bias_second[None]
    )[None]


def solution(mesh):
    in_specs = (
        P("ch", ("grp", "tile")),
        P("tile", None, None),
        P("tile", None, None),
        P("tile", None, None),
        P(),
        P(None, None, "ch", None),
        P("ch"),
        P(),
        P(),
    )
    out_specs = P(("grp", "tile"), "ch", None)
    return jax.shard_map(shards, mesh=mesh, in_specs=in_specs, out_specs=out_specs, check_vma=False)
```

```python
import functools

import jax
import jax.numpy as jnp
from jax import lax
from jax.experimental import pallas as pl
from jax.experimental.pallas import tpu as pltpu
from jax.sharding import PartitionSpec as P

SIDE = 64
TILE_ROW = 4
LANES = 128
MOVES = (TILE_ROW, -1, -TILE_ROW, 1)
BF = jnp.bfloat16
F32 = jnp.float32
SMEM = pl.BlockSpec(memory_space=pltpu.SMEM)
VMEM = pl.BlockSpec(memory_space=pltpu.VMEM)


def fetch_kernel(
    source_ref, wanted_ref, out_ref, other_source, asked, asked_here, table_ref, rows_ref, send_ref,
    side_sems, ask_send, ask_recv, data_send, data_recv, pass_send, pass_recv,
):
    grp, tile, core = (lax.axis_index(name) for name in ("grp", "tile", "ch"))
    tiles = lax.axis_size("tile")
    mesh_id = pl.DeviceIdType.MESH
    sibling = (grp, tile, 1 - core)
    quarter = rows_ref.shape[0]

    def offset(n):
        return 1 + lax.rem(n + tiles // 2 - 1, tiles - 1)

    barrier = pltpu.get_barrier_semaphore()
    pl.semaphore_signal(barrier, inc=1, device_id=sibling, device_id_type=mesh_id)

    def greet(n, carry):
        other = lax.rem(tile + offset(n), tiles)
        pl.semaphore_signal(barrier, inc=1, device_id=(grp, other, core), device_id_type=mesh_id)
        return carry

    lax.fori_loop(0, tiles - 1, greet, 0)
    pl.semaphore_wait(barrier, tiles)

    def remote(src, dst, send_sem, recv_sem, device):
        return pltpu.make_async_remote_copy(
            src_ref=src, dst_ref=dst, send_sem=send_sem, recv_sem=recv_sem,
            device_id=device, device_id_type=mesh_id,
        )

    swap = remote(source_ref, other_source, side_sems.at[0], side_sems.at[1], sibling)
    swap.start()

    def ask_copy(owner, slot, sem_at):
        return remote(
            wanted_ref.at[owner], asked.at[slot], ask_send.at[owner], ask_recv.at[sem_at], (grp, owner, core)
        )

    def ask(n, carry):
        owner = lax.rem(tile + offset(n), tiles)
        ask_copy(owner, tile, tile).start()
        return carry

    lax.fori_loop(0, tiles - 1, ask, 0)
    asked[tile] = wanted_ref[tile]

    def answered(n, carry):
        asker = lax.rem(tile + offset(n), tiles)
        ask_copy(asker, asker, asker).wait_recv()
        return carry

    lax.fori_loop(0, tiles - 1, answered, 0)
    to_scalars = pltpu.make_async_copy(asked, asked_here, side_sems.at[2])
    to_scalars.start()
    swap.wait()
    upper = core == 0
    chans = 2 * source_ref.shape[0]
    cells = source_ref.shape[1]
    span = 512
    spread = (
        lax.broadcasted_iota(jnp.int32, (chans, LANES), 1) % chans
        == lax.broadcasted_iota(jnp.int32, (chans, LANES), 0)
    ).astype(BF)

    def fill(block, carry):
        at = pl.ds(pl.multiple_of(block * span, span), span)
        mine, other = source_ref[:, at].astype(F32), other_source[:, at].astype(F32)
        both = jnp.concatenate([jnp.where(upper, mine, other), jnp.where(upper, other, mine)])
        table_ref[at, :] = lax.dot_general(
            both.astype(BF), spread, (((0,), (0,)), ((), ())), preferred_element_type=F32
        )
        return carry

    lax.fori_loop(0, cells // span, fill, 0)
    to_scalars.wait()
    low = lax.broadcasted_iota(jnp.int32, (1, LANES), 1) < SIDE

    def pick(who):
        def group(g, inner):
            base = g * 16
            for u in range(16):
                left = table_ref[pl.ds(asked_here[who, 0, base + u], 1), :]
                right = table_ref[pl.ds(asked_here[who, 0, base + (quarter + u)], 1), :]
                rows_ref[pl.ds(base + u, 1), :] = jnp.where(low, left, right)
            return inner

        lax.fori_loop(0, quarter // 16, group, 0)
        return rows_ref[...].astype(BF)

    def data_copy(to, slot, sem_at):
        return remote(
            send_ref.at[to], out_ref.at[core, slot], data_send.at[to], data_recv.at[sem_at], (grp, to, core)
        )

    def serve(n, carry):
        asker = lax.rem(tile + offset(n), tiles)
        send_ref[asker] = pick(asker)
        data_copy(asker, tile, tile).start()
        return carry

    lax.fori_loop(0, tiles - 1, serve, 0)
    out_ref[core, tile] = pick(tile)

    def pass_copy(which, owner):
        return remote(
            out_ref.at[which, owner], out_ref.at[which, owner], pass_send.at[owner], pass_recv.at[owner], sibling
        )

    pass_copy(core, tile).start()

    def forward(n, carry):
        owner = lax.rem(tile + tiles - offset(n), tiles)
        data_copy(owner, owner, owner).wait_recv()
        pass_copy(core, owner).start()
        return carry

    lax.fori_loop(0, tiles - 1, forward, 0)

    def close(n, carry):
        pass_copy(core, n).wait_send()
        pass_copy(1 - core, n).wait_recv()
        return carry

    lax.fori_loop(0, tiles, close, 0)

    def close_sends(n, carry):
        other = lax.rem(tile + offset(n), tiles)
        ask_copy(other, other, other).wait_send()
        data_copy(other, other, other).wait_send()
        return carry

    lax.fori_loop(0, tiles - 1, close_sends, 0)


def fetch_rows(source, wanted):
    tiles, _, share = wanted.shape
    quarter = share // 2
    dma = pltpu.SemaphoreType.DMA
    return pl.pallas_call(
        fetch_kernel,
        out_shape=jax.ShapeDtypeStruct((2, tiles, quarter, LANES), BF),
        in_specs=[VMEM, VMEM],
        out_specs=VMEM,
        scratch_shapes=[
            pltpu.VMEM(source.shape, BF),
            pltpu.VMEM(wanted.shape, jnp.int32),
            pltpu.SMEM(wanted.shape, jnp.int32),
            pltpu.VMEM((source.shape[1], LANES), F32),
            pltpu.VMEM((quarter, LANES), F32),
            pltpu.VMEM((tiles, quarter, LANES), BF),
            dma((3,)), dma((tiles,)), dma((tiles,)), dma((tiles,)), dma((tiles,)), dma((tiles,)), dma((tiles,)),
        ],
        compiler_params=pltpu.CompilerParams(
            collective_id=1, has_side_effects=True, vmem_limit_bytes=40 * 2**20
        ),
        name="fetch_rows",
    )(source, wanted)


def remap_kernel(chunk, entries, slots_ref, counts_ref, fetched_ref, out_ref, table_ref, rows_ref):
    part = fetched_ref.shape[0]

    def fill(block, carry):
        at = pl.multiple_of(block * 256, 256)
        piece = fetched_ref[pl.ds(at, 256), :].astype(F32)
        table_ref[pl.ds(at, 256), :] = piece
        table_ref[pl.ds(part + at, 256), :] = pltpu.roll(piece, SIDE, 1)
        return carry

    lax.fori_loop(0, part // 256, fill, 0)
    cells = out_ref.shape[0]

    def step(block, carry):
        base = block * chunk

        def group(g, inner):
            first = (base + g * 8) * entries
            for u in range(8):
                for k in range(entries):
                    rows_ref[k, pl.ds(g * 8 + u, 1), :] = table_ref[pl.ds(slots_ref[first + (u * entries + k)], 1), :]
            return inner

        lax.fori_loop(0, chunk // 8, group, 0)
        here = pl.ds(pl.multiple_of(base, chunk), chunk)
        weights = counts_ref[here, :]
        count = weights[:, 0:1]
        summed = weights[:, 0:1] * rows_ref[0]
        for k in range(1, entries):
            count = count + weights[:, k : k + 1]
            summed = summed + weights[:, k : k + 1] * rows_ref[k]
        out_ref[here, :] = (summed / count)[:, :SIDE].astype(BF)
        return carry

    lax.fori_loop(0, cells // chunk, step, 0)


def remap_cells(slots, counts, fetched):
    cells, entries = counts.shape
    chunk = 128
    return pl.pallas_call(
        functools.partial(remap_kernel, chunk, entries),
        out_shape=jax.ShapeDtypeStruct((cells, SIDE), BF),
        in_specs=[SMEM, VMEM, VMEM],
        out_specs=VMEM,
        scratch_shapes=[
            pltpu.VMEM((2 * fetched.shape[0], LANES), F32),
            pltpu.VMEM((entries, chunk, LANES), F32),
        ],
        compiler_params=pltpu.CompilerParams(vmem_limit_bytes=40 * 2**20),
        name="remap_cells",
    )(slots, counts, fetched)


def seam_choice(seam, position, core, height):
    tiles = seam.shape[0]
    place = jnp.arange(SIDE, dtype=jnp.int32)
    rows = []
    for side, by in enumerate(MOVES):
        code = lax.dynamic_index_in_dim(seam, (position + by) % tiles, 0, keepdims=False)[side]
        edge = code % 4
        cell = jnp.where(code >= 4, SIDE - 1 - place, place)
        near = cell - core * height
        column = jnp.where((near >= 0) & (near < height), 2 * SIDE + jnp.where(edge == 1, height, 0) + near, -1)
        row = jnp.where(core == edge // 2, core * SIDE + cell, -1)
        rows.append(jnp.where(edge % 2 == 0, row, column))
    wanted = jnp.concatenate(rows)
    width = 2 * SIDE + 2 * height
    return (wanted[:, None] == jnp.arange(width, dtype=jnp.int32)[None, :]).astype(BF)


def block_kernel(
    half_ref, choice_ref, first_ref, first_bias_ref, second_ref, second_bias_ref, out_ref,
    field, hidden, west_buf, east_buf, left_shift, right_shift, mid_buf, pack_one, pack_two,
    send_one, send_two, recv_one, recv_two, halo_one, halo_two, other_first, other_bias,
    first_full, turned, send_sems, recv_sems, side_sems,
):
    grp, tile, core = (lax.axis_index(name) for name in ("grp", "tile", "ch"))
    tiles = lax.axis_size("tile")
    sibling = (grp, tile, 1 - core)
    upper = core == 0
    cells = half_ref.shape[0]
    height = cells // SIDE
    rows = cells + 2 * SIDE
    start = 8
    body = start + SIDE
    targets = [lax.rem(tile + by + tiles, tiles) for by in MOVES]
    sources = [lax.rem(tile - by + tiles, tiles) for by in MOVES]

    barrier = pltpu.get_barrier_semaphore()
    pl.semaphore_signal(barrier, inc=1, device_id=sibling, device_id_type=pl.DeviceIdType.MESH)
    for other in targets:
        for c in range(2):
            pl.semaphore_signal(barrier, inc=1, device_id=(grp, other, c), device_id_type=pl.DeviceIdType.MESH)

    field[pl.ds(body, cells), :] = half_ref[...].astype(F32)
    pl.semaphore_wait(barrier, 9)

    def remote(src, dst, send_sem, recv_sem, device):
        return pltpu.make_async_remote_copy(
            src_ref=src, dst_ref=dst, send_sem=send_sem, recv_sem=recv_sem,
            device_id=device, device_id_type=pl.DeviceIdType.MESH,
        )

    def begin(rnd, grid, pack, send, recv, halo):
        pack[0:SIDE, :] = grid[body : body + SIDE, :].astype(BF)
        pack[SIDE : 2 * SIDE, :] = grid[body + cells - SIDE : body + cells, :].astype(BF)
        a = 2 * SIDE
        pack[a : a + height, :] = grid[pl.ds(body, height, stride=SIDE), :].astype(BF)
        pack[a + height : a + 2 * height, :] = grid[pl.ds(body + SIDE - 1, height, stride=SIDE), :].astype(BF)
        rims = jnp.dot(choice_ref[...], pack[...], preferred_element_type=F32).astype(BF)
        for d in range(4):
            send[d] = rims[d * SIDE : (d + 1) * SIDE]
        copies = []
        for d in range(4):
            for c in range(2):
                copies.append(
                    remote(
                        send.at[d], recv.at[core, d], send_sems.at[rnd, 2 * d + c],
                        recv_sems.at[rnd, core * 4 + d], (grp, targets[d], c),
                    )
                )
        inner = pl.multiple_of((1 - core) * SIDE, SIDE)
        copies.append(
            remote(pack.at[pl.ds(inner, SIDE), :], halo, send_sems.at[rnd, 8], recv_sems.at[rnd, 8], sibling)
        )
        for copy in copies:
            copy.start()
        return copies

    def finish(rnd, copies, grid, send, recv, halo, left, right, mid, width):
        lanes = slice(0, width)
        for d in range(4):
            for c in range(2):
                remote(
                    send.at[d], recv.at[c, d], send_sems.at[rnd, 2 * d + c],
                    recv_sems.at[rnd, c * 4 + d], (grp, sources[d], c),
                ).wait_recv()
        copies[-1].wait_recv()
        north, east, south, west = [recv[0, d].astype(F32) + recv[1, d].astype(F32) for d in range(4)]
        inside = halo[...].astype(F32)
        grid[start:body, :] = jnp.where(upper, north, inside)
        grid[body + cells : body + cells + SIDE, :] = jnp.where(upper, inside, south)

        def corner(one, two):
            return ((one + two) * 0.5).astype(BF).astype(F32)

        def column(buf, rim, place):
            buf[8 : 8 + SIDE, lanes] = rim
            buf[7:8, lanes] = corner(north[place : place + 1], rim[0:1])
            buf[8 + SIDE : 9 + SIDE, lanes] = corner(south[place : place + 1], rim[SIDE - 1 : SIDE])
            return jnp.where(
                upper, buf[7 : 9 + height, lanes], buf[7 + SIDE - height : 9 + SIDE, lanes]
            )

        west_cells = column(west_buf, west, 0)
        east_cells = column(east_buf, east, SIDE - 1)
        left[...] = grid[start - 1 : start - 1 + rows, :]
        left[pl.ds(0, height + 2, stride=SIDE), :] = west_cells
        right[...] = grid[start + 1 : start + 1 + rows, :]
        right[pl.ds(SIDE - 1, height + 2, stride=SIDE), :] = east_cells
        mid[0, :, lanes] = left[...].astype(BF)
        mid[1, :, lanes] = grid[start : start + rows, :].astype(BF)
        mid[2, :, lanes] = right[...].astype(BF)
        for copy in copies:
            copy.wait_send()

    block = 256

    def convolve(mid, weights, at, width):
        total = None
        for a in range(3):
            for b in range(3):
                piece = mid[b, pl.ds(pl.multiple_of(at + a * SIDE, SIDE), block), 0:width]
                term = jnp.dot(piece, weights[3 * a + b], preferred_element_type=F32)
                total = term if total is None else total + term
        return total

    weight_copy = remote(first_ref, other_first, side_sems.at[0], side_sems.at[1], sibling)
    bias_copy = remote(first_bias_ref, other_bias, side_sems.at[2], side_sems.at[3], sibling)
    copies = begin(0, field, pack_one, send_one, recv_one, halo_one)
    weight_copy.start()
    bias_copy.start()
    weight_copy.wait()
    bias_copy.wait()
    mine, other = first_ref[...], other_first[...]
    first_full[:, :, 0:SIDE] = jnp.where(upper, mine, other)
    first_full[:, :, SIDE:] = jnp.where(upper, other, mine)
    mine, other = first_bias_ref[0:1, :], other_bias[0:1, :]
    bias = jnp.concatenate([jnp.where(upper, mine, other), jnp.where(upper, other, mine)], axis=1)
    finish(0, copies, field, send_one, recv_one, halo_one, left_shift[0], right_shift[0], mid_buf, SIDE)

    def first(step, carry):
        at = pl.multiple_of(step * block, block)
        v = convolve(mid_buf, first_full, at, SIDE) + bias
        act = 0.5 * v * (1.0 + jnp.tanh(0.7978845608028654 * (v + 0.044715 * (v * v * v))))
        hidden[pl.ds(pl.multiple_of(body + at, 8), block), :] = act.astype(BF).astype(F32)
        return carry

    lax.fori_loop(0, cells // block, first, 0)
    copies = begin(1, hidden, pack_two, send_two, recv_two, halo_two)
    finish(1, copies, hidden, send_two, recv_two, halo_two, left_shift[1], right_shift[1], mid_buf, 2 * SIDE)

    def second(step, carry):
        at = pl.multiple_of(step * block, block)
        v = convolve(mid_buf, second_ref, at, 2 * SIDE) + second_bias_ref[...]
        v = v + field[pl.ds(pl.multiple_of(body + at, 8), block), :]
        turned[:, pl.ds(at, block)] = v.T.astype(BF)
        return carry

    lax.fori_loop(0, cells // block, second, 0)
    share = SIDE // 2
    away = remote(
        turned.at[pl.ds(pl.multiple_of((1 - core) * share, share), share), :],
        out_ref.at[:, pl.ds(pl.multiple_of(core * cells, cells), cells)],
        side_sems.at[4], side_sems.at[5], sibling,
    )
    away.start()
    out_ref[:, pl.ds(pl.multiple_of(core * cells, cells), cells)] = turned[
        pl.ds(pl.multiple_of(core * share, share), share), :
    ]
    away.wait()


def conv_block(half, choice, first, first_bias, second, second_bias):
    cells, chans = half.shape
    hid = 2 * chans
    rows = cells + 2 * SIDE
    pack = choice.shape[1]
    shape = pltpu.VMEM

    def kernel(*refs):
        ins, rest = refs[:7], list(refs[7:])
        l1, l2, r1, r2 = rest[4:8]
        block_kernel(*ins, *rest[:4], (l1, l2), (r1, r2), *rest[8:])

    return pl.pallas_call(
        kernel,
        out_shape=jax.ShapeDtypeStruct((chans // 2, 2 * cells), BF),
        in_specs=[VMEM] * 6,
        out_specs=VMEM,
        scratch_shapes=[
            shape((rows + 16, chans), F32), shape((rows + 16, hid), F32),
            shape((SIDE + 16, hid), F32), shape((SIDE + 16, hid), F32),
            shape((rows, chans), F32), shape((rows, hid), F32),
            shape((rows, chans), F32), shape((rows, hid), F32),
            shape((3, rows, hid), BF),
            shape((pack, chans), BF), shape((pack, hid), BF),
            shape((4, SIDE, chans), BF), shape((4, SIDE, hid), BF),
            shape((2, 4, SIDE, chans), BF), shape((2, 4, SIDE, hid), BF),
            shape((SIDE, chans), BF), shape((SIDE, hid), BF),
            shape(first.shape, BF), shape(first_bias.shape, F32),
            shape((9, chans, hid), BF), shape((chans, cells), BF),
            pltpu.SemaphoreType.DMA((2, 9)), pltpu.SemaphoreType.DMA((2, 9)), pltpu.SemaphoreType.DMA((6,)),
        ],
        compiler_params=pltpu.CompilerParams(
            collective_id=0, has_side_effects=True, vmem_limit_bytes=48 * 2**20
        ),
        name="conv_block",
    )(half, choice, first, first_bias, second, second_bias)


def shards(source, request_rows, cell_slots, cell_counts, seam, conv_first, bias_first, conv_second, bias_second):
    position = lax.axis_index("tile")
    core = lax.axis_index("ch")
    tiles, slots_each = request_rows.shape[1], request_rows.shape[2]
    share = slots_each // 2
    quarter = share // 2
    cells_half = cell_slots.shape[2] // 2

    requests = lax.dynamic_slice_in_dim(request_rows[0], core * share, share, 1)
    fetched = fetch_rows(source, requests[:, None, :]).reshape(2 * tiles * quarter, LANES)

    slots = lax.dynamic_slice_in_dim(cell_slots[0], core * cells_half, cells_half, 1)
    counts = lax.dynamic_slice_in_dim(cell_counts[0], core * cells_half, cells_half, 1)
    owner, place = slots // slots_each, slots % slots_each
    served, inside = place // share, place % share
    part = tiles * quarter
    table_rows = (inside // quarter) * (2 * part) + served * part + owner * quarter + inside % quarter
    remapped = remap_cells(table_rows.T.reshape(-1), counts.astype(F32).T, fetched)

    choice = seam_choice(seam, position, core, cells_half // SIDE)

    def arrange(weights):
        return jnp.transpose(weights, (0, 1, 3, 2)).reshape(9, weights.shape[3], weights.shape[2])

    bias_rows = jnp.broadcast_to(bias_first[None], (8, bias_first.shape[0]))
    return conv_block(
        remapped, choice, arrange(conv_first), bias_rows, arrange(conv_second), bias_second[None]
    )[None]


def solution(mesh):
    in_specs = (
        P("ch", ("grp", "tile")),
        P("tile", None, None),
        P("tile", None, None),
        P("tile", None, None),
        P(),
        P(None, None, "ch", None),
        P("ch"),
        P(),
        P(),
    )
    out_specs = P(("grp", "tile"), "ch", None)
    return jax.shard_map(shards, mesh=mesh, in_specs=in_specs, out_specs=out_specs, check_vma=False)
```

```python
import functools

import jax
import jax.numpy as jnp
from jax import lax
from jax.experimental import pallas as pl
from jax.experimental.pallas import tpu as pltpu
from jax.sharding import PartitionSpec as P

SIDE = 64
TILE_ROW = 4
LANES = 128
MOVES = (TILE_ROW, -1, -TILE_ROW, 1)
BF = jnp.bfloat16
F32 = jnp.float32
SMEM = pl.BlockSpec(memory_space=pltpu.SMEM)
VMEM = pl.BlockSpec(memory_space=pltpu.VMEM)


def fetch_kernel(
    source_ref, wanted_ref, out_ref, other_source, asked, asked_here, table_ref, rows_ref, send_ref,
    side_sems, ask_send, ask_recv, data_send, data_recv, pass_send, pass_recv,
):
    grp, tile, core = (lax.axis_index(name) for name in ("grp", "tile", "ch"))
    tiles = lax.axis_size("tile")
    mesh_id = pl.DeviceIdType.MESH
    sibling = (grp, tile, 1 - core)
    quarter = rows_ref.shape[0]

    middle = tiles // 2
    side_start = tile // middle * middle
    across = middle - side_start
    place = lax.rem(tile, middle)

    def partner(n, sign=1):
        far = 1 - n // middle
        base = far * across + (1 - far) * side_start
        return base + lax.rem(place + middle + sign * (lax.rem(n, middle) + 1 - far), middle)

    barrier = pltpu.get_barrier_semaphore()
    pl.semaphore_signal(barrier, inc=1, device_id=sibling, device_id_type=mesh_id)

    def greet(n, carry):
        other = partner(n)
        pl.semaphore_signal(barrier, inc=1, device_id=(grp, other, core), device_id_type=mesh_id)
        return carry

    lax.fori_loop(0, tiles - 1, greet, 0)
    pl.semaphore_wait(barrier, tiles)

    def remote(src, dst, send_sem, recv_sem, device):
        return pltpu.make_async_remote_copy(
            src_ref=src, dst_ref=dst, send_sem=send_sem, recv_sem=recv_sem,
            device_id=device, device_id_type=mesh_id,
        )

    swap = remote(source_ref, other_source, side_sems.at[0], side_sems.at[1], sibling)
    swap.start()

    def ask_copy(owner, slot, sem_at):
        return remote(
            wanted_ref.at[owner], asked.at[slot], ask_send.at[owner], ask_recv.at[sem_at], (grp, owner, core)
        )

    def ask(n, carry):
        owner = partner(n)
        ask_copy(owner, tile, tile).start()
        return carry

    lax.fori_loop(0, tiles - 1, ask, 0)
    asked[tile] = wanted_ref[tile]

    def answered(n, carry):
        asker = partner(n)
        ask_copy(asker, asker, asker).wait_recv()
        return carry

    lax.fori_loop(0, tiles - 1, answered, 0)
    to_scalars = pltpu.make_async_copy(asked, asked_here, side_sems.at[2])
    to_scalars.start()
    swap.wait()
    upper = core == 0
    chans = 2 * source_ref.shape[0]
    cells = source_ref.shape[1]
    span = 512
    spread = (
        lax.broadcasted_iota(jnp.int32, (chans, LANES), 1) % chans
        == lax.broadcasted_iota(jnp.int32, (chans, LANES), 0)
    ).astype(BF)

    def fill(block, carry):
        at = pl.ds(pl.multiple_of(block * span, span), span)
        mine, other = source_ref[:, at].astype(F32), other_source[:, at].astype(F32)
        both = jnp.concatenate([jnp.where(upper, mine, other), jnp.where(upper, other, mine)])
        table_ref[at, :] = lax.dot_general(
            both.astype(BF), spread, (((0,), (0,)), ((), ())), preferred_element_type=F32
        )
        return carry

    lax.fori_loop(0, cells // span, fill, 0)
    to_scalars.wait()
    low = lax.broadcasted_iota(jnp.int32, (1, LANES), 1) < SIDE

    def pick(who):
        def group(g, inner):
            base = g * 16
            for u in range(16):
                left = table_ref[pl.ds(asked_here[who, 0, base + u], 1), :]
                right = table_ref[pl.ds(asked_here[who, 0, base + (quarter + u)], 1), :]
                rows_ref[pl.ds(base + u, 1), :] = jnp.where(low, left, right)
            return inner

        lax.fori_loop(0, quarter // 16, group, 0)
        return rows_ref[...].astype(BF)

    def data_copy(to, slot, sem_at):
        return remote(
            send_ref.at[to], out_ref.at[core, slot], data_send.at[to], data_recv.at[sem_at], (grp, to, core)
        )

    def serve(n, carry):
        asker = partner(n)
        send_ref[asker] = pick(asker)
        data_copy(asker, tile, tile).start()
        return carry

    lax.fori_loop(0, tiles - 1, serve, 0)
    out_ref[core, tile] = pick(tile)

    def pass_copy(which, owner):
        return remote(
            out_ref.at[which, owner], out_ref.at[which, owner], pass_send.at[owner], pass_recv.at[owner], sibling
        )

    pass_copy(core, tile).start()

    def forward(n, carry):
        owner = partner(n, -1)
        data_copy(owner, owner, owner).wait_recv()
        pass_copy(core, owner).start()
        return carry

    lax.fori_loop(0, tiles - 1, forward, 0)

    def close(n, carry):
        pass_copy(core, n).wait_send()
        pass_copy(1 - core, n).wait_recv()
        return carry

    lax.fori_loop(0, tiles, close, 0)

    def close_sends(n, carry):
        other = partner(n)
        ask_copy(other, other, other).wait_send()
        data_copy(other, other, other).wait_send()
        return carry

    lax.fori_loop(0, tiles - 1, close_sends, 0)


def fetch_rows(source, wanted):
    tiles, _, share = wanted.shape
    quarter = share // 2
    dma = pltpu.SemaphoreType.DMA
    return pl.pallas_call(
        fetch_kernel,
        out_shape=jax.ShapeDtypeStruct((2, tiles, quarter, LANES), BF),
        in_specs=[VMEM, VMEM],
        out_specs=VMEM,
        scratch_shapes=[
            pltpu.VMEM(source.shape, BF),
            pltpu.VMEM(wanted.shape, jnp.int32),
            pltpu.SMEM(wanted.shape, jnp.int32),
            pltpu.VMEM((source.shape[1], LANES), F32),
            pltpu.VMEM((quarter, LANES), F32),
            pltpu.VMEM((tiles, quarter, LANES), BF),
            dma((3,)), dma((tiles,)), dma((tiles,)), dma((tiles,)), dma((tiles,)), dma((tiles,)), dma((tiles,)),
        ],
        compiler_params=pltpu.CompilerParams(
            collective_id=1, has_side_effects=True, vmem_limit_bytes=40 * 2**20
        ),
        name="fetch_rows",
    )(source, wanted)


def remap_into(chunk, entries, slots_ref, counts_ref, fetched_ref, field, body, table_ref, rows_ref):
    part = fetched_ref.shape[0]

    def fill(block, carry):
        at = pl.multiple_of(block * 256, 256)
        piece = fetched_ref[pl.ds(at, 256), :].astype(F32)
        table_ref[pl.ds(at, 256), :] = piece
        table_ref[pl.ds(part + at, 256), :] = pltpu.roll(piece, SIDE, 1)
        return carry

    lax.fori_loop(0, part // 256, fill, 0)
    cells = counts_ref.shape[0]

    def step(block, carry):
        base = block * chunk

        def group(g, inner):
            first = (base + g * 8) * entries
            for u in range(8):
                for k in range(entries):
                    rows_ref[k, pl.ds(g * 8 + u, 1), :] = table_ref[pl.ds(slots_ref[first + (u * entries + k)], 1), :]
            return inner

        lax.fori_loop(0, chunk // 8, group, 0)
        weights = counts_ref[pl.ds(pl.multiple_of(base, chunk), chunk), :]
        count = weights[:, 0:1]
        summed = weights[:, 0:1] * rows_ref[0]
        for k in range(1, entries):
            count = count + weights[:, k : k + 1]
            summed = summed + weights[:, k : k + 1] * rows_ref[k]
        cell = (summed / count)[:, :SIDE].astype(BF).astype(F32)
        field[pl.ds(pl.multiple_of(body + base, 8), chunk), :] = cell
        return carry

    lax.fori_loop(0, cells // chunk, step, 0)


def choose_edges(codes, core, height, width, choice):
    i = lax.broadcasted_iota(jnp.int32, (SIDE, width), 0)
    lane = lax.broadcasted_iota(jnp.int32, (SIDE, width), 1)
    for d, code in enumerate(codes):
        flip = code // 4
        edge = code % 4
        is_column = edge % 2
        second = edge // 2
        cell = i + flip * (SIDE - 1 - 2 * i)
        near = cell - core * height
        in_column = (lane == near + (2 * SIDE + (1 - second) * height)) & (near >= 0) & (near < height)
        in_row = lane == cell + core * SIDE
        row_here = (1 - is_column) * (second * core + (1 - second) * (1 - core))
        hit = in_column.astype(jnp.int32) * is_column + in_row.astype(jnp.int32) * row_here
        choice[d * SIDE : (d + 1) * SIDE, :] = hit.astype(F32).astype(BF)


def block_kernel(
    slots_ref, counts_ref, fetched_ref, seam_ref, first_ref, first_bias_ref, second_ref, second_bias_ref, out_ref,
    table_ref, rows_ref, choice_ref,
    field, hidden, west_buf, east_buf, left_shift, right_shift, mid_buf, pack_one, pack_two,
    send_one, send_two, recv_one, recv_two, halo_one, halo_two, other_first, other_bias,
    first_full, turned, send_sems, recv_sems, side_sems,
):
    grp, tile, core = (lax.axis_index(name) for name in ("grp", "tile", "ch"))
    tiles = lax.axis_size("tile")
    sibling = (grp, tile, 1 - core)
    upper = core == 0
    cells = counts_ref.shape[0]
    height = cells // SIDE
    rows = cells + 2 * SIDE
    start = 8
    body = start + SIDE
    targets = [lax.rem(tile + by + tiles, tiles) for by in MOVES]
    sources = [lax.rem(tile - by + tiles, tiles) for by in MOVES]

    barrier = pltpu.get_barrier_semaphore()
    pl.semaphore_signal(barrier, inc=1, device_id=sibling, device_id_type=pl.DeviceIdType.MESH)
    for other in targets:
        for c in range(2):
            pl.semaphore_signal(barrier, inc=1, device_id=(grp, other, c), device_id_type=pl.DeviceIdType.MESH)

    codes = [seam_ref[targets[d], d] for d in range(4)]
    choose_edges(codes, core, height, choice_ref.shape[1], choice_ref)
    entries = counts_ref.shape[1]
    remap_into(128, entries, slots_ref, counts_ref, fetched_ref, field, body, table_ref, rows_ref)
    pl.semaphore_wait(barrier, 9)

    def remote(src, dst, send_sem, recv_sem, device):
        return pltpu.make_async_remote_copy(
            src_ref=src, dst_ref=dst, send_sem=send_sem, recv_sem=recv_sem,
            device_id=device, device_id_type=pl.DeviceIdType.MESH,
        )

    def begin(rnd, grid, pack, send, recv, halo):
        pack[0:SIDE, :] = grid[body : body + SIDE, :].astype(BF)
        pack[SIDE : 2 * SIDE, :] = grid[body + cells - SIDE : body + cells, :].astype(BF)
        a = 2 * SIDE
        pack[a : a + height, :] = grid[pl.ds(body, height, stride=SIDE), :].astype(BF)
        pack[a + height : a + 2 * height, :] = grid[pl.ds(body + SIDE - 1, height, stride=SIDE), :].astype(BF)
        rims = jnp.dot(choice_ref[...], pack[...], preferred_element_type=F32).astype(BF)
        for d in range(4):
            send[d] = rims[d * SIDE : (d + 1) * SIDE]
        copies = []
        for d in range(4):
            for c in range(2):
                copies.append(
                    remote(
                        send.at[d], recv.at[core, d], send_sems.at[rnd, 2 * d + c],
                        recv_sems.at[rnd, core * 4 + d], (grp, targets[d], c),
                    )
                )
        inner = pl.multiple_of((1 - core) * SIDE, SIDE)
        copies.append(
            remote(pack.at[pl.ds(inner, SIDE), :], halo, send_sems.at[rnd, 8], recv_sems.at[rnd, 8], sibling)
        )
        for copy in copies:
            copy.start()
        return copies

    def prepare(grid, left, right, mid, width):
        left[SIDE : SIDE + cells, :] = grid[body - 1 : body - 1 + cells, :]
        right[SIDE : SIDE + cells, :] = grid[body + 1 : body + 1 + cells, :]
        mid[1, SIDE : SIDE + cells, 0:width] = grid[body : body + cells, :].astype(BF)

    def finish(rnd, copies, grid, send, recv, halo, left, right, mid, width):
        lanes = slice(0, width)
        for d in range(4):
            for c in range(2):
                remote(
                    send.at[d], recv.at[c, d], send_sems.at[rnd, 2 * d + c],
                    recv_sems.at[rnd, c * 4 + d], (grp, sources[d], c),
                ).wait_recv()
        copies[-1].wait_recv()
        north, east, south, west = [recv[0, d].astype(F32) + recv[1, d].astype(F32) for d in range(4)]
        inside = halo[...].astype(F32)
        grid[start:body, :] = jnp.where(upper, north, inside)
        grid[body + cells : body + cells + SIDE, :] = jnp.where(upper, inside, south)

        def corner(one, two):
            return ((one + two) * 0.5).astype(BF).astype(F32)

        def column(buf, rim, place):
            buf[8 : 8 + SIDE, lanes] = rim
            buf[7:8, lanes] = corner(north[place : place + 1], rim[0:1])
            buf[8 + SIDE : 9 + SIDE, lanes] = corner(south[place : place + 1], rim[SIDE - 1 : SIDE])
            return jnp.where(
                upper, buf[7 : 9 + height, lanes], buf[7 + SIDE - height : 9 + SIDE, lanes]
            )

        west_cells = column(west_buf, west, 0)
        east_cells = column(east_buf, east, SIDE - 1)
        for at in (0, SIDE + cells):
            left[at : at + SIDE, :] = grid[start + at - 1 : start + at - 1 + SIDE, :]
            right[at : at + SIDE, :] = grid[start + at + 1 : start + at + 1 + SIDE, :]
            mid[1, at : at + SIDE, lanes] = grid[start + at : start + at + SIDE, :].astype(BF)
        left[pl.ds(0, height + 2, stride=SIDE), :] = west_cells
        right[pl.ds(SIDE - 1, height + 2, stride=SIDE), :] = east_cells
        mid[0, :, lanes] = left[...].astype(BF)
        mid[2, :, lanes] = right[...].astype(BF)
        for copy in copies:
            copy.wait_send()

    block = 256

    def convolve(mid, weights, at, width):
        total = None
        for a in range(3):
            for b in range(3):
                piece = mid[b, pl.ds(pl.multiple_of(at + a * SIDE, SIDE), block), 0:width]
                term = jnp.dot(piece, weights[3 * a + b], preferred_element_type=F32)
                total = term if total is None else total + term
        return total

    weight_copy = remote(first_ref, other_first, side_sems.at[0], side_sems.at[1], sibling)
    bias_copy = remote(first_bias_ref, other_bias, side_sems.at[2], side_sems.at[3], sibling)
    weight_copy.start()
    bias_copy.start()
    copies = begin(0, field, pack_one, send_one, recv_one, halo_one)
    prepare(field, left_shift[0], right_shift[0], mid_buf, SIDE)
    weight_copy.wait()
    bias_copy.wait()
    mine, other = first_ref[...], other_first[...]
    first_full[:, :, 0:SIDE] = jnp.where(upper, mine, other)
    first_full[:, :, SIDE:] = jnp.where(upper, other, mine)
    mine, other = first_bias_ref[0:1, :], other_bias[0:1, :]
    bias = jnp.concatenate([jnp.where(upper, mine, other), jnp.where(upper, other, mine)], axis=1)
    finish(0, copies, field, send_one, recv_one, halo_one, left_shift[0], right_shift[0], mid_buf, SIDE)

    def first(step, carry):
        at = pl.multiple_of(step * block, block)
        v = convolve(mid_buf, first_full, at, SIDE) + bias
        act = 0.5 * v * (1.0 + jnp.tanh(0.7978845608028654 * (v + 0.044715 * (v * v * v))))
        hidden[pl.ds(pl.multiple_of(body + at, 8), block), :] = act.astype(BF).astype(F32)
        return carry

    lax.fori_loop(0, cells // block, first, 0)
    copies = begin(1, hidden, pack_two, send_two, recv_two, halo_two)
    prepare(hidden, left_shift[1], right_shift[1], mid_buf, 2 * SIDE)
    finish(1, copies, hidden, send_two, recv_two, halo_two, left_shift[1], right_shift[1], mid_buf, 2 * SIDE)

    def second(step, carry):
        at = pl.multiple_of(step * block, block)
        v = convolve(mid_buf, second_ref, at, 2 * SIDE) + second_bias_ref[...]
        v = v + field[pl.ds(pl.multiple_of(body + at, 8), block), :]
        turned[:, pl.ds(at, block)] = v.T.astype(BF)
        return carry

    lax.fori_loop(0, cells // block, second, 0)
    share = SIDE // 2
    away = remote(
        turned.at[pl.ds(pl.multiple_of((1 - core) * share, share), share), :],
        out_ref.at[:, pl.ds(pl.multiple_of(core * cells, cells), cells)],
        side_sems.at[4], side_sems.at[5], sibling,
    )
    away.start()
    out_ref[:, pl.ds(pl.multiple_of(core * cells, cells), cells)] = turned[
        pl.ds(pl.multiple_of(core * share, share), share), :
    ]
    away.wait()


def conv_block(slots, counts, fetched, seam, first, first_bias, second, second_bias):
    cells, entries = counts.shape
    chans = first.shape[1]
    hid = 2 * chans
    rows = cells + 2 * SIDE
    pack = 2 * SIDE + 2 * (cells // SIDE)
    shape = pltpu.VMEM

    def kernel(*refs):
        ins, rest = refs[:12], list(refs[12:])
        l1, l2, r1, r2 = rest[4:8]
        block_kernel(*ins, *rest[:4], (l1, l2), (r1, r2), *rest[8:])

    return pl.pallas_call(
        kernel,
        out_shape=jax.ShapeDtypeStruct((chans // 2, 2 * cells), BF),
        in_specs=[SMEM, VMEM, VMEM, SMEM, VMEM, VMEM, VMEM, VMEM],
        out_specs=VMEM,
        scratch_shapes=[
            shape((2 * fetched.shape[0], LANES), F32), shape((entries, 128, LANES), F32),
            shape((4 * SIDE, pack), BF),
            shape((rows + 16, chans), F32), shape((rows + 16, hid), F32),
            shape((SIDE + 16, hid), F32), shape((SIDE + 16, hid), F32),
            shape((rows, chans), F32), shape((rows, hid), F32),
            shape((rows, chans), F32), shape((rows, hid), F32),
            shape((3, rows, hid), BF),
            shape((pack, chans), BF), shape((pack, hid), BF),
            shape((4, SIDE, chans), BF), shape((4, SIDE, hid), BF),
            shape((2, 4, SIDE, chans), BF), shape((2, 4, SIDE, hid), BF),
            shape((SIDE, chans), BF), shape((SIDE, hid), BF),
            shape(first.shape, BF), shape(first_bias.shape, F32),
            shape((9, chans, hid), BF), shape((chans, cells), BF),
            pltpu.SemaphoreType.DMA((2, 9)), pltpu.SemaphoreType.DMA((2, 9)), pltpu.SemaphoreType.DMA((6,)),
        ],
        compiler_params=pltpu.CompilerParams(
            collective_id=0, has_side_effects=True, vmem_limit_bytes=48 * 2**20
        ),
        name="conv_block",
    )(slots, counts, fetched, seam, first, first_bias, second, second_bias)


def shards(source, request_rows, cell_slots, cell_counts, seam, conv_first, bias_first, conv_second, bias_second):
    core = lax.axis_index("ch")
    tiles, slots_each = request_rows.shape[1], request_rows.shape[2]
    share = slots_each // 2
    quarter = share // 2
    cells_half = cell_slots.shape[2] // 2

    requests = lax.dynamic_slice_in_dim(request_rows[0], core * share, share, 1)
    fetched = fetch_rows(source, requests[:, None, :]).reshape(2 * tiles * quarter, LANES)

    slots = lax.dynamic_slice_in_dim(cell_slots[0], core * cells_half, cells_half, 1)
    counts = lax.dynamic_slice_in_dim(cell_counts[0], core * cells_half, cells_half, 1)
    owner, place = slots // slots_each, slots % slots_each
    served, inside = place // share, place % share
    part = tiles * quarter
    table_rows = (inside // quarter) * (2 * part) + served * part + owner * quarter + inside % quarter
    def arrange(weights):
        return jnp.transpose(weights, (0, 1, 3, 2)).reshape(9, weights.shape[3], weights.shape[2])

    bias_rows = jnp.broadcast_to(bias_first[None], (8, bias_first.shape[0]))
    return conv_block(
        table_rows.T.reshape(-1), counts.astype(F32).T, fetched, seam,
        arrange(conv_first), bias_rows, arrange(conv_second), bias_second[None],
    )[None]


def solution(mesh):
    in_specs = (
        P("ch", ("grp", "tile")),
        P("tile", None, None),
        P("tile", None, None),
        P("tile", None, None),
        P(),
        P(None, None, "ch", None),
        P("ch"),
        P(),
        P(),
    )
    out_specs = P(("grp", "tile"), "ch", None)
    return jax.shard_map(shards, mesh=mesh, in_specs=in_specs, out_specs=out_specs, check_vma=False)
```

```python
import functools

import jax
import jax.numpy as jnp
from jax import lax
from jax.experimental import pallas as pl
from jax.experimental.pallas import tpu as pltpu
from jax.sharding import PartitionSpec as P

SIDE = 64
TILE_ROW = 4
LANES = 128
MOVES = (TILE_ROW, -1, -TILE_ROW, 1)
BF = jnp.bfloat16
F32 = jnp.float32
SMEM = pl.BlockSpec(memory_space=pltpu.SMEM)
VMEM = pl.BlockSpec(memory_space=pltpu.VMEM)


def fetch_kernel(
    source_ref, wanted_ref, out_ref, other_source, asked, asked_here, table_ref, rows_ref, send_ref,
    side_sems, ask_send, ask_recv, data_send, data_recv, pass_send, pass_recv,
):
    grp, tile, core = (lax.axis_index(name) for name in ("grp", "tile", "ch"))
    tiles = lax.axis_size("tile")
    mesh_id = pl.DeviceIdType.MESH
    sibling = (grp, tile, 1 - core)
    quarter = rows_ref.shape[0]

    middle = tiles // 2
    side_start = tile // middle * middle
    across = middle - side_start
    place = lax.rem(tile, middle)

    def partner(n, sign=1):
        far = 1 - n // middle
        base = far * across + (1 - far) * side_start
        return base + lax.rem(place + middle + sign * (lax.rem(n, middle) + 1 - far), middle)

    barrier = pltpu.get_barrier_semaphore()
    pl.semaphore_signal(barrier, inc=1, device_id=sibling, device_id_type=mesh_id)

    def greet(n, carry):
        other = partner(n)
        pl.semaphore_signal(barrier, inc=1, device_id=(grp, other, core), device_id_type=mesh_id)
        return carry

    lax.fori_loop(0, tiles - 1, greet, 0)
    pl.semaphore_wait(barrier, tiles)

    def remote(src, dst, send_sem, recv_sem, device):
        return pltpu.make_async_remote_copy(
            src_ref=src, dst_ref=dst, send_sem=send_sem, recv_sem=recv_sem,
            device_id=device, device_id_type=mesh_id,
        )

    swap = remote(source_ref, other_source, side_sems.at[0], side_sems.at[1], sibling)
    swap.start()

    def ask_copy(owner, slot, sem_at):
        return remote(
            wanted_ref.at[owner], asked.at[slot], ask_send.at[owner], ask_recv.at[sem_at], (grp, owner, core)
        )

    def ask(n, carry):
        owner = partner(n)
        ask_copy(owner, tile, tile).start()
        return carry

    lax.fori_loop(0, tiles - 1, ask, 0)
    asked[tile] = wanted_ref[tile]

    def answered(n, carry):
        asker = partner(n)
        ask_copy(asker, asker, asker).wait_recv()
        return carry

    lax.fori_loop(0, tiles - 1, answered, 0)
    to_scalars = pltpu.make_async_copy(asked, asked_here, side_sems.at[2])
    to_scalars.start()
    swap.wait()
    upper = core == 0
    chans = 2 * source_ref.shape[0]
    cells = source_ref.shape[1]
    span = 512
    spread = (
        lax.broadcasted_iota(jnp.int32, (chans, LANES), 1) % chans
        == lax.broadcasted_iota(jnp.int32, (chans, LANES), 0)
    ).astype(BF)

    def fill(block, carry):
        at = pl.ds(pl.multiple_of(block * span, span), span)
        mine, other = source_ref[:, at].astype(F32), other_source[:, at].astype(F32)
        both = jnp.concatenate([jnp.where(upper, mine, other), jnp.where(upper, other, mine)])
        table_ref[at, :] = lax.dot_general(
            both.astype(BF), spread, (((0,), (0,)), ((), ())), preferred_element_type=F32
        )
        return carry

    lax.fori_loop(0, cells // span, fill, 0)
    to_scalars.wait()
    low = lax.broadcasted_iota(jnp.int32, (1, LANES), 1) < SIDE

    def pick(who):
        def group(g, inner):
            base = g * 16
            for u in range(16):
                left = table_ref[pl.ds(asked_here[who, 0, base + u], 1), :]
                right = table_ref[pl.ds(asked_here[who, 0, base + (quarter + u)], 1), :]
                rows_ref[pl.ds(base + u, 1), :] = jnp.where(low, left, right)
            return inner

        lax.fori_loop(0, quarter // 16, group, 0)
        return rows_ref[...].astype(BF)

    def data_copy(to, slot, sem_at):
        return remote(
            send_ref.at[to], out_ref.at[core, slot], data_send.at[to], data_recv.at[sem_at], (grp, to, core)
        )

    def serve(n, carry):
        asker = partner(n)
        send_ref[asker] = pick(asker)
        data_copy(asker, tile, tile).start()
        return carry

    lax.fori_loop(0, tiles - 1, serve, 0)
    out_ref[core, tile] = pick(tile)

    def pass_copy(which, owner):
        return remote(
            out_ref.at[which, owner], out_ref.at[which, owner], pass_send.at[owner], pass_recv.at[owner], sibling
        )

    pass_copy(core, tile).start()

    def forward(n, carry):
        owner = partner(n, -1)
        data_copy(owner, owner, owner).wait_recv()
        pass_copy(core, owner).start()
        return carry

    lax.fori_loop(0, tiles - 1, forward, 0)

    def close(n, carry):
        pass_copy(core, n).wait_send()
        pass_copy(1 - core, n).wait_recv()
        return carry

    lax.fori_loop(0, tiles, close, 0)

    def close_sends(n, carry):
        other = partner(n)
        ask_copy(other, other, other).wait_send()
        data_copy(other, other, other).wait_send()
        return carry

    lax.fori_loop(0, tiles - 1, close_sends, 0)


def fetch_rows(source, wanted):
    tiles, _, share = wanted.shape
    quarter = share // 2
    dma = pltpu.SemaphoreType.DMA
    return pl.pallas_call(
        fetch_kernel,
        out_shape=jax.ShapeDtypeStruct((2, tiles, quarter, LANES), BF),
        in_specs=[VMEM, VMEM],
        out_specs=VMEM,
        scratch_shapes=[
            pltpu.VMEM(source.shape, BF),
            pltpu.VMEM(wanted.shape, jnp.int32),
            pltpu.SMEM(wanted.shape, jnp.int32),
            pltpu.VMEM((source.shape[1], LANES), F32),
            pltpu.VMEM((quarter, LANES), F32),
            pltpu.VMEM((tiles, quarter, LANES), BF),
            dma((3,)), dma((tiles,)), dma((tiles,)), dma((tiles,)), dma((tiles,)), dma((tiles,)), dma((tiles,)),
        ],
        compiler_params=pltpu.CompilerParams(
            collective_id=1, has_side_effects=True, vmem_limit_bytes=40 * 2**20
        ),
        name="fetch_rows",
    )(source, wanted)


def remap_into(chunk, entries, slots_copy, slots_here, counts_ref, fetched_ref, field, body, table_ref, rows_ref):
    part = fetched_ref.shape[0]

    def fill(block, carry):
        at = pl.multiple_of(block * 256, 256)
        piece = fetched_ref[pl.ds(at, 256), :].astype(F32)
        table_ref[pl.ds(at, 256), :] = piece
        table_ref[pl.ds(part + at, 256), :] = pltpu.roll(piece, SIDE, 1)
        return carry

    lax.fori_loop(0, part // 256, fill, 0)
    slots_copy.wait()
    cells = counts_ref.shape[0]

    def step(block, carry):
        base = block * chunk

        def group(g, inner):
            first = base + g * 8
            for u in range(8):
                for k in range(entries):
                    rows_ref[k, pl.ds(g * 8 + u, 1), :] = table_ref[pl.ds(slots_here[k, 0, first + u], 1), :]
            return inner

        lax.fori_loop(0, chunk // 8, group, 0)
        weights = counts_ref[pl.ds(pl.multiple_of(base, chunk), chunk), :]
        count = weights[:, 0:1]
        summed = weights[:, 0:1] * rows_ref[0]
        for k in range(1, entries):
            count = count + weights[:, k : k + 1]
            summed = summed + weights[:, k : k + 1] * rows_ref[k]
        cell = (summed / count)[:, :SIDE].astype(BF).astype(F32)
        field[pl.ds(pl.multiple_of(body + base, 8), chunk), :] = cell
        return carry

    lax.fori_loop(0, cells // chunk, step, 0)


def choose_edges(codes, core, height, width, choice):
    i = lax.broadcasted_iota(jnp.int32, (SIDE, width), 0)
    lane = lax.broadcasted_iota(jnp.int32, (SIDE, width), 1)
    for d, code in enumerate(codes):
        flip = code // 4
        edge = code % 4
        is_column = edge % 2
        second = edge // 2
        cell = i + flip * (SIDE - 1 - 2 * i)
        near = cell - core * height
        in_column = (lane == near + (2 * SIDE + (1 - second) * height)) & (near >= 0) & (near < height)
        in_row = lane == cell + core * SIDE
        row_here = (1 - is_column) * (second * core + (1 - second) * (1 - core))
        hit = in_column.astype(jnp.int32) * is_column + in_row.astype(jnp.int32) * row_here
        choice[d * SIDE : (d + 1) * SIDE, :] = hit.astype(F32).astype(BF)


def block_kernel(
    cap,
    slots_ref, counts_ref, fetched_ref, seam_ref, first_ref, first_bias_ref, second_ref, second_bias_ref, out_ref,
    table_ref, rows_ref, choice_ref, slots_moved, slots_here, second_full,
    field, hidden, west_buf, east_buf, left_shift, right_shift, mid_buf, pack_one, pack_two,
    send_one, send_two, recv_one, recv_two, halo_one, halo_two, other_first, other_bias,
    first_full, turned, send_sems, recv_sems, side_sems,
):
    grp, tile, core = (lax.axis_index(name) for name in ("grp", "tile", "ch"))
    tiles = lax.axis_size("tile")
    sibling = (grp, tile, 1 - core)
    upper = core == 0
    cells = counts_ref.shape[0]
    height = cells // SIDE
    rows = cells + 2 * SIDE
    start = 8
    body = start + SIDE
    targets = [lax.rem(tile + by + tiles, tiles) for by in MOVES]
    sources = [lax.rem(tile - by + tiles, tiles) for by in MOVES]

    barrier = pltpu.get_barrier_semaphore()
    pl.semaphore_signal(barrier, inc=1, device_id=sibling, device_id_type=pl.DeviceIdType.MESH)
    slot = slots_ref[:, pl.ds(pl.multiple_of(core * cells, cells), cells)]
    part = fetched_ref.shape[0]
    owner, inside = slot // cap, slot % cap
    served, inside = inside // (cap // 2), inside % (cap // 2)
    group, inside = inside // (cap // 4), inside % (cap // 4)
    at_row = group * part + served * (part // 2) + owner * (cap // 4) + inside
    for k in range(slots_ref.shape[0]):
        slots_moved[k] = at_row[k : k + 1]
    slots_copy = pltpu.make_async_copy(slots_moved, slots_here, side_sems.at[6])
    slots_copy.start()
    for other in targets:
        for c in range(2):
            pl.semaphore_signal(barrier, inc=1, device_id=(grp, other, c), device_id_type=pl.DeviceIdType.MESH)

    codes = [seam_ref[targets[d], d] for d in range(4)]
    choose_edges(codes, core, height, choice_ref.shape[1], choice_ref)
    entries = counts_ref.shape[1]
    for k in range(9):
        second_full[k] = second_ref[k].astype(F32).T.astype(BF)
    remap_into(128, entries, slots_copy, slots_here, counts_ref, fetched_ref, field, body, table_ref, rows_ref)
    pl.semaphore_wait(barrier, 9)

    def remote(src, dst, send_sem, recv_sem, device):
        return pltpu.make_async_remote_copy(
            src_ref=src, dst_ref=dst, send_sem=send_sem, recv_sem=recv_sem,
            device_id=device, device_id_type=pl.DeviceIdType.MESH,
        )

    def begin(rnd, grid, pack, send, recv, halo):
        pack[0:SIDE, :] = grid[body : body + SIDE, :].astype(BF)
        pack[SIDE : 2 * SIDE, :] = grid[body + cells - SIDE : body + cells, :].astype(BF)
        a = 2 * SIDE
        pack[a : a + height, :] = grid[pl.ds(body, height, stride=SIDE), :].astype(BF)
        pack[a + height : a + 2 * height, :] = grid[pl.ds(body + SIDE - 1, height, stride=SIDE), :].astype(BF)
        rims = jnp.dot(choice_ref[...], pack[...], preferred_element_type=F32).astype(BF)
        for d in range(4):
            send[d] = rims[d * SIDE : (d + 1) * SIDE]
        copies = []
        for d in range(4):
            for c in range(2):
                copies.append(
                    remote(
                        send.at[d], recv.at[core, d], send_sems.at[rnd, 2 * d + c],
                        recv_sems.at[rnd, core * 4 + d], (grp, targets[d], c),
                    )
                )
        inner = pl.multiple_of((1 - core) * SIDE, SIDE)
        copies.append(
            remote(pack.at[pl.ds(inner, SIDE), :], halo, send_sems.at[rnd, 8], recv_sems.at[rnd, 8], sibling)
        )
        for copy in copies:
            copy.start()
        return copies

    def prepare(grid, left, right, mid, width):
        left[SIDE : SIDE + cells, :] = grid[body - 1 : body - 1 + cells, :]
        right[SIDE : SIDE + cells, :] = grid[body + 1 : body + 1 + cells, :]
        mid[1, SIDE : SIDE + cells, 0:width] = grid[body : body + cells, :].astype(BF)

    def finish(rnd, copies, grid, send, recv, halo, left, right, mid, width):
        lanes = slice(0, width)
        for d in range(4):
            for c in range(2):
                remote(
                    send.at[d], recv.at[c, d], send_sems.at[rnd, 2 * d + c],
                    recv_sems.at[rnd, c * 4 + d], (grp, sources[d], c),
                ).wait_recv()
        copies[-1].wait_recv()
        north, east, south, west = [recv[0, d].astype(F32) + recv[1, d].astype(F32) for d in range(4)]
        inside = halo[...].astype(F32)
        grid[start:body, :] = jnp.where(upper, north, inside)
        grid[body + cells : body + cells + SIDE, :] = jnp.where(upper, inside, south)

        def corner(one, two):
            return ((one + two) * 0.5).astype(BF).astype(F32)

        def column(buf, rim, place):
            buf[8 : 8 + SIDE, lanes] = rim
            buf[7:8, lanes] = corner(north[place : place + 1], rim[0:1])
            buf[8 + SIDE : 9 + SIDE, lanes] = corner(south[place : place + 1], rim[SIDE - 1 : SIDE])
            return jnp.where(
                upper, buf[7 : 9 + height, lanes], buf[7 + SIDE - height : 9 + SIDE, lanes]
            )

        west_cells = column(west_buf, west, 0)
        east_cells = column(east_buf, east, SIDE - 1)
        for at in (0, SIDE + cells):
            left[at : at + SIDE, :] = grid[start + at - 1 : start + at - 1 + SIDE, :]
            right[at : at + SIDE, :] = grid[start + at + 1 : start + at + 1 + SIDE, :]
            mid[1, at : at + SIDE, lanes] = grid[start + at : start + at + SIDE, :].astype(BF)
        left[pl.ds(0, height + 2, stride=SIDE), :] = west_cells
        right[pl.ds(SIDE - 1, height + 2, stride=SIDE), :] = east_cells
        mid[0, :, lanes] = left[...].astype(BF)
        mid[2, :, lanes] = right[...].astype(BF)
        for copy in copies:
            copy.wait_send()

    block = 256

    def convolve(mid, weights, at, width):
        total = None
        for a in range(3):
            for b in range(3):
                piece = mid[b, pl.ds(pl.multiple_of(at + a * SIDE, SIDE), block), 0:width]
                term = jnp.dot(piece, weights[3 * a + b], preferred_element_type=F32)
                total = term if total is None else total + term
        return total

    weight_copy = remote(first_ref, other_first, side_sems.at[0], side_sems.at[1], sibling)
    bias_copy = remote(first_bias_ref, other_bias, side_sems.at[2], side_sems.at[3], sibling)
    weight_copy.start()
    bias_copy.start()
    copies = begin(0, field, pack_one, send_one, recv_one, halo_one)
    prepare(field, left_shift[0], right_shift[0], mid_buf, SIDE)
    weight_copy.wait()
    bias_copy.wait()
    mine, other = first_ref[...], other_first[...]
    for k in range(9):
        one, two = mine[k].astype(F32), other[k].astype(F32)
        both = jnp.concatenate([jnp.where(upper, one, two), jnp.where(upper, two, one)])
        first_full[k] = both.T.astype(BF)
    mine, other = first_bias_ref[...], other_bias[...]
    bias = jnp.concatenate([jnp.where(upper, mine, other), jnp.where(upper, other, mine)], axis=1)
    finish(0, copies, field, send_one, recv_one, halo_one, left_shift[0], right_shift[0], mid_buf, SIDE)

    def first(step, carry):
        at = pl.multiple_of(step * block, block)
        v = convolve(mid_buf, first_full, at, SIDE) + bias
        act = 0.5 * v * (1.0 + jnp.tanh(0.7978845608028654 * (v + 0.044715 * (v * v * v))))
        hidden[pl.ds(pl.multiple_of(body + at, 8), block), :] = act.astype(BF).astype(F32)
        return carry

    lax.fori_loop(0, cells // block, first, 0)
    copies = begin(1, hidden, pack_two, send_two, recv_two, halo_two)
    prepare(hidden, left_shift[1], right_shift[1], mid_buf, 2 * SIDE)
    finish(1, copies, hidden, send_two, recv_two, halo_two, left_shift[1], right_shift[1], mid_buf, 2 * SIDE)

    def second(step, carry):
        at = pl.multiple_of(step * block, block)
        v = convolve(mid_buf, second_full, at, 2 * SIDE) + second_bias_ref[...]
        v = v + field[pl.ds(pl.multiple_of(body + at, 8), block), :]
        turned[:, pl.ds(at, block)] = v.T.astype(BF)
        return carry

    lax.fori_loop(0, cells // block, second, 0)
    share = SIDE // 2
    away = remote(
        turned.at[pl.ds(pl.multiple_of((1 - core) * share, share), share), :],
        out_ref.at[:, pl.ds(pl.multiple_of(core * cells, cells), cells)],
        side_sems.at[4], side_sems.at[5], sibling,
    )
    away.start()
    out_ref[:, pl.ds(pl.multiple_of(core * cells, cells), cells)] = turned[
        pl.ds(pl.multiple_of(core * share, share), share), :
    ]
    away.wait()


def conv_block(cap, slots, counts, fetched, seam, first, first_bias, second, second_bias):
    cells, entries = counts.shape
    chans = first.shape[2]
    hid = 2 * chans
    rows = cells + 2 * SIDE
    pack = 2 * SIDE + 2 * (cells // SIDE)
    shape = pltpu.VMEM

    def kernel(*refs):
        ins, rest = refs[:15], list(refs[15:])
        l1, l2, r1, r2 = rest[4:8]
        block_kernel(cap, *ins, *rest[:4], (l1, l2), (r1, r2), *rest[8:])

    return pl.pallas_call(
        kernel,
        out_shape=jax.ShapeDtypeStruct((chans // 2, 2 * cells), BF),
        in_specs=[VMEM, VMEM, VMEM, SMEM, VMEM, VMEM, VMEM, VMEM],
        out_specs=VMEM,
        scratch_shapes=[
            shape((2 * fetched.shape[0], LANES), F32), shape((entries, 128, LANES), F32),
            shape((4 * SIDE, pack), BF), shape((entries, 1, cells), jnp.int32),
            pltpu.SMEM((entries, 1, cells), jnp.int32), shape((9, hid, chans), BF),
            shape((rows + 16, chans), F32), shape((rows + 16, hid), F32),
            shape((SIDE + 16, hid), F32), shape((SIDE + 16, hid), F32),
            shape((rows, chans), F32), shape((rows, hid), F32),
            shape((rows, chans), F32), shape((rows, hid), F32),
            shape((3, rows, hid), BF),
            shape((pack, chans), BF), shape((pack, hid), BF),
            shape((4, SIDE, chans), BF), shape((4, SIDE, hid), BF),
            shape((2, 4, SIDE, chans), BF), shape((2, 4, SIDE, hid), BF),
            shape((SIDE, chans), BF), shape((SIDE, hid), BF),
            shape(first.shape, BF), shape(first_bias.shape, F32),
            shape((9, chans, hid), BF), shape((chans, cells), BF),
            pltpu.SemaphoreType.DMA((2, 9)), pltpu.SemaphoreType.DMA((2, 9)), pltpu.SemaphoreType.DMA((7,)),
        ],
        compiler_params=pltpu.CompilerParams(
            collective_id=0, has_side_effects=True, vmem_limit_bytes=48 * 2**20
        ),
        name="conv_block",
    )(slots, counts, fetched, seam, first, first_bias, second, second_bias)


def shards(source, request_rows, cell_slots, cell_counts, seam, conv_first, bias_first, conv_second, bias_second):
    core = lax.axis_index("ch")
    tiles, slots_each = request_rows.shape[1], request_rows.shape[2]
    share = slots_each // 2
    quarter = share // 2
    cells_half = cell_slots.shape[2] // 2

    requests = lax.dynamic_slice_in_dim(request_rows[0], core * share, share, 1)
    fetched = fetch_rows(source, requests[:, None, :]).reshape(2 * tiles * quarter, LANES)

    counts = lax.dynamic_slice_in_dim(cell_counts[0], core * cells_half, cells_half, 1)
    def taps(weights):
        return weights.reshape(9, weights.shape[2], weights.shape[3])

    return conv_block(
        slots_each, cell_slots[0], counts.astype(F32).T, fetched, seam,
        taps(conv_first), bias_first[None], taps(conv_second), bias_second[None],
    )[None]


def solution(mesh):
    in_specs = (
        P("ch", ("grp", "tile")),
        P("tile", None, None),
        P("tile", None, None),
        P("tile", None, None),
        P(),
        P(None, None, "ch", None),
        P("ch"),
        P(),
        P(),
    )
    out_specs = P(("grp", "tile"), "ch", None)
    return jax.shard_map(shards, mesh=mesh, in_specs=in_specs, out_specs=out_specs, check_vma=False)
```

```python
import functools

import jax
import jax.numpy as jnp
from jax import lax
from jax.experimental import pallas as pl
from jax.experimental.pallas import tpu as pltpu
from jax.sharding import PartitionSpec as P

SIDE = 64
TILE_ROW = 4
LANES = 128
MOVES = (TILE_ROW, -1, -TILE_ROW, 1)
BF = jnp.bfloat16
F32 = jnp.float32
SMEM = pl.BlockSpec(memory_space=pltpu.SMEM)
VMEM = pl.BlockSpec(memory_space=pltpu.VMEM)


def fetch_kernel(
    source_ref, wanted_ref, out_ref, other_source, asked, asked_here, table_ref, rows_ref, send_ref,
    side_sems, ask_send, ask_recv, data_send, data_recv, pass_send, pass_recv,
):
    grp, tile, core = (lax.axis_index(name) for name in ("grp", "tile", "ch"))
    tiles = lax.axis_size("tile")
    mesh_id = pl.DeviceIdType.MESH
    sibling = (grp, tile, 1 - core)
    quarter = rows_ref.shape[0]

    middle = tiles // 2
    side_start = tile // middle * middle
    across = middle - side_start
    place = lax.rem(tile, middle)

    def partner(n, sign=1):
        far = 1 - n // middle
        base = far * across + (1 - far) * side_start
        return base + lax.rem(place + middle + sign * (lax.rem(n, middle) + 1 - far), middle)

    barrier = pltpu.get_barrier_semaphore()
    pl.semaphore_signal(barrier, inc=1, device_id=sibling, device_id_type=mesh_id)

    def greet(n, carry):
        other = partner(n)
        pl.semaphore_signal(barrier, inc=1, device_id=(grp, other, core), device_id_type=mesh_id)
        return carry

    lax.fori_loop(0, tiles - 1, greet, 0)
    pl.semaphore_wait(barrier, tiles)

    def remote(src, dst, send_sem, recv_sem, device):
        return pltpu.make_async_remote_copy(
            src_ref=src, dst_ref=dst, send_sem=send_sem, recv_sem=recv_sem,
            device_id=device, device_id_type=mesh_id,
        )

    swap = remote(source_ref, other_source, side_sems.at[0], side_sems.at[1], sibling)
    swap.start()

    def ask_copy(owner, slot, sem_at):
        return remote(
            wanted_ref.at[owner], asked.at[slot], ask_send.at[owner], ask_recv.at[sem_at], (grp, owner, core)
        )

    def ask(n, carry):
        owner = partner(n)
        ask_copy(owner, tile, tile).start()
        return carry

    lax.fori_loop(0, tiles - 1, ask, 0)
    asked[tile] = wanted_ref[tile]

    def answered(n, carry):
        asker = partner(n)
        ask_copy(asker, asker, asker).wait_recv()
        return carry

    lax.fori_loop(0, tiles - 1, answered, 0)
    to_scalars = pltpu.make_async_copy(asked, asked_here, side_sems.at[2])
    to_scalars.start()
    swap.wait()
    upper = core == 0
    chans = 2 * source_ref.shape[0]
    cells = source_ref.shape[1]
    span = 512
    spread = (
        lax.broadcasted_iota(jnp.int32, (chans, LANES), 1) % chans
        == lax.broadcasted_iota(jnp.int32, (chans, LANES), 0)
    ).astype(BF)

    def fill(block, carry):
        at = pl.ds(pl.multiple_of(block * span, span), span)
        mine, other = source_ref[:, at].astype(F32), other_source[:, at].astype(F32)
        both = jnp.concatenate([jnp.where(upper, mine, other), jnp.where(upper, other, mine)])
        table_ref[at, :] = lax.dot_general(
            both.astype(BF), spread, (((0,), (0,)), ((), ())), preferred_element_type=F32
        )
        return carry

    lax.fori_loop(0, cells // span, fill, 0)
    to_scalars.wait()
    low = lax.broadcasted_iota(jnp.int32, (1, LANES), 1) < SIDE

    def pick(who):
        def group(g, inner):
            base = g * 16
            for u in range(16):
                left = table_ref[pl.ds(asked_here[who, 0, base + u], 1), :]
                right = table_ref[pl.ds(asked_here[who, 0, base + (quarter + u)], 1), :]
                rows_ref[pl.ds(base + u, 1), :] = jnp.where(low, left, right)
            return inner

        lax.fori_loop(0, quarter // 16, group, 0)
        return rows_ref[...].astype(BF)

    def data_copy(to, slot, sem_at):
        return remote(
            send_ref.at[to], out_ref.at[core, slot], data_send.at[to], data_recv.at[sem_at], (grp, to, core)
        )

    def serve(n, carry):
        asker = partner(n)
        send_ref[asker] = pick(asker)
        data_copy(asker, tile, tile).start()
        return carry

    lax.fori_loop(0, tiles - 1, serve, 0)
    out_ref[core, tile] = pick(tile)

    def pass_copy(which, owner):
        return remote(
            out_ref.at[which, owner], out_ref.at[which, owner], pass_send.at[owner], pass_recv.at[owner], sibling
        )

    pass_copy(core, tile).start()

    def forward(n, carry):
        owner = partner(n, -1)
        data_copy(owner, owner, owner).wait_recv()
        pass_copy(core, owner).start()
        return carry

    lax.fori_loop(0, tiles - 1, forward, 0)

    def close(n, carry):
        pass_copy(core, n).wait_send()
        pass_copy(1 - core, n).wait_recv()
        return carry

    lax.fori_loop(0, tiles, close, 0)

    def close_sends(n, carry):
        other = partner(n)
        ask_copy(other, other, other).wait_send()
        data_copy(other, other, other).wait_send()
        return carry

    lax.fori_loop(0, tiles - 1, close_sends, 0)


def fetch_rows(source, wanted):
    tiles, _, share = wanted.shape
    quarter = share // 2
    dma = pltpu.SemaphoreType.DMA
    return pl.pallas_call(
        fetch_kernel,
        out_shape=jax.ShapeDtypeStruct((2, tiles, quarter, LANES), BF),
        in_specs=[VMEM, VMEM],
        out_specs=VMEM,
        scratch_shapes=[
            pltpu.VMEM(source.shape, BF),
            pltpu.VMEM(wanted.shape, jnp.int32),
            pltpu.SMEM(wanted.shape, jnp.int32),
            pltpu.VMEM((source.shape[1], LANES), F32),
            pltpu.VMEM((quarter, LANES), F32),
            pltpu.VMEM((tiles, quarter, LANES), BF),
            dma((3,)), dma((tiles,)), dma((tiles,)), dma((tiles,)), dma((tiles,)), dma((tiles,)), dma((tiles,)),
        ],
        compiler_params=pltpu.CompilerParams(
            collective_id=1, has_side_effects=True, vmem_limit_bytes=40 * 2**20
        ),
        name="fetch_rows",
    )(source, wanted)


def remap_into(chunk, entries, slots_copy, slots_here, counts_ref, fetched_ref, field, body, table_ref, rows_ref):
    part = fetched_ref.shape[0]

    def fill(block, carry):
        at = pl.multiple_of(block * 256, 256)
        piece = fetched_ref[pl.ds(at, 256), :].astype(F32)
        table_ref[pl.ds(at, 256), :] = piece
        table_ref[pl.ds(part + at, 256), :] = pltpu.roll(piece, SIDE, 1)
        return carry

    lax.fori_loop(0, part // 256, fill, 0)
    slots_copy.wait()
    cells = counts_ref.shape[0]

    def step(block, carry):
        base = block * chunk

        def group(g, inner):
            first = base + g * 8
            for u in range(8):
                for k in range(entries):
                    rows_ref[k, pl.ds(g * 8 + u, 1), :] = table_ref[pl.ds(slots_here[first + (k * cells + u)], 1), :]
            return inner

        lax.fori_loop(0, chunk // 8, group, 0)
        weights = counts_ref[pl.ds(pl.multiple_of(base, chunk), chunk), :]
        count = weights[:, 0:1]
        summed = weights[:, 0:1] * rows_ref[0]
        for k in range(1, entries):
            count = count + weights[:, k : k + 1]
            summed = summed + weights[:, k : k + 1] * rows_ref[k]
        cell = (summed / count)[:, :SIDE].astype(BF).astype(F32)
        field[pl.ds(pl.multiple_of(body + base, 8), chunk), :] = cell
        return carry

    lax.fori_loop(0, cells // chunk, step, 0)


def choose_edges(codes, core, height, width, choice):
    i = lax.broadcasted_iota(jnp.int32, (SIDE, width), 0)
    lane = lax.broadcasted_iota(jnp.int32, (SIDE, width), 1)
    for d, code in enumerate(codes):
        flip = code // 4
        edge = code % 4
        is_column = edge % 2
        second = edge // 2
        cell = i + flip * (SIDE - 1 - 2 * i)
        near = cell - core * height
        in_column = (lane == near + (2 * SIDE + (1 - second) * height)) & (near >= 0) & (near < height)
        in_row = lane == cell + core * SIDE
        row_here = (1 - is_column) * (second * core + (1 - second) * (1 - core))
        hit = in_column.astype(jnp.int32) * is_column + in_row.astype(jnp.int32) * row_here
        choice[d * SIDE : (d + 1) * SIDE, :] = hit.astype(F32).astype(BF)


def block_kernel(
    cap,
    slots_ref, counts_ref, fetched_ref, seam_ref, first_ref, first_bias_ref, second_ref, second_bias_ref, out_ref,
    table_ref, rows_ref, choice_ref, slots_moved, slots_here, second_full,
    field, hidden, west_buf, east_buf, left_shift, right_shift, mid_buf, pack_one, pack_two,
    send_one, send_two, recv_one, recv_two, halo_one, halo_two, other_first, other_bias,
    first_full, turned, send_sems, recv_sems, side_sems,
):
    grp, tile, core = (lax.axis_index(name) for name in ("grp", "tile", "ch"))
    tiles = lax.axis_size("tile")
    sibling = (grp, tile, 1 - core)
    upper = core == 0
    cells = counts_ref.shape[0]
    height = cells // SIDE
    rows = cells + 2 * SIDE
    start = 8
    body = start + SIDE
    targets = [lax.rem(tile + by + tiles, tiles) for by in MOVES]
    sources = [lax.rem(tile - by + tiles, tiles) for by in MOVES]

    barrier = pltpu.get_barrier_semaphore()
    pl.semaphore_signal(barrier, inc=1, device_id=sibling, device_id_type=pl.DeviceIdType.MESH)
    slot = slots_ref[:, pl.ds(pl.multiple_of(core * cells, cells), cells)]
    part = fetched_ref.shape[0]
    owner, inside = slot // cap, slot % cap
    served, inside = inside // (cap // 2), inside % (cap // 2)
    group, inside = inside // (cap // 4), inside % (cap // 4)
    at_row = group * part + served * (part // 2) + owner * (cap // 4) + inside
    for k in range(slots_ref.shape[0]):
        slots_moved[k * cells : (k + 1) * cells] = at_row[k]
    slots_copy = pltpu.make_async_copy(slots_moved, slots_here, side_sems.at[6])
    slots_copy.start()
    for other in targets:
        for c in range(2):
            pl.semaphore_signal(barrier, inc=1, device_id=(grp, other, c), device_id_type=pl.DeviceIdType.MESH)

    codes = [seam_ref[targets[d], d] for d in range(4)]
    choose_edges(codes, core, height, choice_ref.shape[1], choice_ref)
    entries = counts_ref.shape[1]
    for k in range(9):
        second_full[k] = second_ref[k].astype(F32).T.astype(BF)
    remap_into(128, entries, slots_copy, slots_here, counts_ref, fetched_ref, field, body, table_ref, rows_ref)
    pl.semaphore_wait(barrier, 9)

    def remote(src, dst, send_sem, recv_sem, device):
        return pltpu.make_async_remote_copy(
            src_ref=src, dst_ref=dst, send_sem=send_sem, recv_sem=recv_sem,
            device_id=device, device_id_type=pl.DeviceIdType.MESH,
        )

    def begin(rnd, grid, pack, send, recv, halo):
        pack[0:SIDE, :] = grid[body : body + SIDE, :].astype(BF)
        pack[SIDE : 2 * SIDE, :] = grid[body + cells - SIDE : body + cells, :].astype(BF)
        a = 2 * SIDE
        pack[a : a + height, :] = grid[pl.ds(body, height, stride=SIDE), :].astype(BF)
        pack[a + height : a + 2 * height, :] = grid[pl.ds(body + SIDE - 1, height, stride=SIDE), :].astype(BF)
        rims = jnp.dot(choice_ref[...], pack[...], preferred_element_type=F32).astype(BF)
        for d in range(4):
            send[d] = rims[d * SIDE : (d + 1) * SIDE]
        copies = []
        for d in range(4):
            for c in range(2):
                copies.append(
                    remote(
                        send.at[d], recv.at[core, d], send_sems.at[rnd, 2 * d + c],
                        recv_sems.at[rnd, core * 4 + d], (grp, targets[d], c),
                    )
                )
        inner = pl.multiple_of((1 - core) * SIDE, SIDE)
        copies.append(
            remote(pack.at[pl.ds(inner, SIDE), :], halo, send_sems.at[rnd, 8], recv_sems.at[rnd, 8], sibling)
        )
        for copy in copies:
            copy.start()
        return copies

    def prepare(grid, left, right, mid, width):
        left[SIDE : SIDE + cells, :] = grid[body - 1 : body - 1 + cells, :]
        right[SIDE : SIDE + cells, :] = grid[body + 1 : body + 1 + cells, :]
        mid[1, SIDE : SIDE + cells, 0:width] = grid[body : body + cells, :].astype(BF)

    def finish(rnd, copies, grid, send, recv, halo, left, right, mid, width):
        lanes = slice(0, width)
        for d in range(4):
            for c in range(2):
                remote(
                    send.at[d], recv.at[c, d], send_sems.at[rnd, 2 * d + c],
                    recv_sems.at[rnd, c * 4 + d], (grp, sources[d], c),
                ).wait_recv()
        copies[-1].wait_recv()
        north, east, south, west = [recv[0, d].astype(F32) + recv[1, d].astype(F32) for d in range(4)]
        inside = halo[...].astype(F32)
        grid[start:body, :] = jnp.where(upper, north, inside)
        grid[body + cells : body + cells + SIDE, :] = jnp.where(upper, inside, south)

        def corner(one, two):
            return ((one + two) * 0.5).astype(BF).astype(F32)

        def column(buf, rim, place):
            buf[8 : 8 + SIDE, lanes] = rim
            buf[7:8, lanes] = corner(north[place : place + 1], rim[0:1])
            buf[8 + SIDE : 9 + SIDE, lanes] = corner(south[place : place + 1], rim[SIDE - 1 : SIDE])
            return jnp.where(
                upper, buf[7 : 9 + height, lanes], buf[7 + SIDE - height : 9 + SIDE, lanes]
            )

        west_cells = column(west_buf, west, 0)
        east_cells = column(east_buf, east, SIDE - 1)
        for at in (0, SIDE + cells):
            left[at : at + SIDE, :] = grid[start + at - 1 : start + at - 1 + SIDE, :]
            right[at : at + SIDE, :] = grid[start + at + 1 : start + at + 1 + SIDE, :]
            mid[1, at : at + SIDE, lanes] = grid[start + at : start + at + SIDE, :].astype(BF)
        left[pl.ds(0, height + 2, stride=SIDE), :] = west_cells
        right[pl.ds(SIDE - 1, height + 2, stride=SIDE), :] = east_cells
        mid[0, :, lanes] = left[...].astype(BF)
        mid[2, :, lanes] = right[...].astype(BF)
        for copy in copies:
            copy.wait_send()

    block = 256

    def convolve(mid, weights, at, width):
        total = None
        for a in range(3):
            for b in range(3):
                piece = mid[b, pl.ds(pl.multiple_of(at + a * SIDE, SIDE), block), 0:width]
                term = jnp.dot(piece, weights[3 * a + b], preferred_element_type=F32)
                total = term if total is None else total + term
        return total

    weight_copy = remote(first_ref, other_first, side_sems.at[0], side_sems.at[1], sibling)
    bias_copy = remote(first_bias_ref, other_bias, side_sems.at[2], side_sems.at[3], sibling)
    weight_copy.start()
    bias_copy.start()
    copies = begin(0, field, pack_one, send_one, recv_one, halo_one)
    prepare(field, left_shift[0], right_shift[0], mid_buf, SIDE)
    weight_copy.wait()
    bias_copy.wait()
    mine, other = first_ref[...], other_first[...]
    for k in range(9):
        one, two = mine[k].astype(F32), other[k].astype(F32)
        both = jnp.concatenate([jnp.where(upper, one, two), jnp.where(upper, two, one)])
        first_full[k] = both.T.astype(BF)
    mine, other = first_bias_ref[...], other_bias[...]
    bias = jnp.concatenate([jnp.where(upper, mine, other), jnp.where(upper, other, mine)], axis=1)
    finish(0, copies, field, send_one, recv_one, halo_one, left_shift[0], right_shift[0], mid_buf, SIDE)

    def first(step, carry):
        at = pl.multiple_of(step * block, block)
        v = convolve(mid_buf, first_full, at, SIDE) + bias
        act = 0.5 * v * (1.0 + jnp.tanh(0.7978845608028654 * (v + 0.044715 * (v * v * v))))
        hidden[pl.ds(pl.multiple_of(body + at, 8), block), :] = act.astype(BF).astype(F32)
        return carry

    lax.fori_loop(0, cells // block, first, 0)
    copies = begin(1, hidden, pack_two, send_two, recv_two, halo_two)
    prepare(hidden, left_shift[1], right_shift[1], mid_buf, 2 * SIDE)
    finish(1, copies, hidden, send_two, recv_two, halo_two, left_shift[1], right_shift[1], mid_buf, 2 * SIDE)

    def second(step, carry):
        at = pl.multiple_of(step * block, block)
        v = convolve(mid_buf, second_full, at, 2 * SIDE) + second_bias_ref[...]
        v = v + field[pl.ds(pl.multiple_of(body + at, 8), block), :]
        turned[:, pl.ds(at, block)] = v.T.astype(BF)
        return carry

    lax.fori_loop(0, cells // block, second, 0)
    share = SIDE // 2
    away = remote(
        turned.at[pl.ds(pl.multiple_of((1 - core) * share, share), share), :],
        out_ref.at[:, pl.ds(pl.multiple_of(core * cells, cells), cells)],
        side_sems.at[4], side_sems.at[5], sibling,
    )
    away.start()
    out_ref[:, pl.ds(pl.multiple_of(core * cells, cells), cells)] = turned[
        pl.ds(pl.multiple_of(core * share, share), share), :
    ]
    away.wait()


def conv_block(cap, slots, counts, fetched, seam, first, first_bias, second, second_bias):
    cells, entries = counts.shape
    chans = first.shape[2]
    hid = 2 * chans
    rows = cells + 2 * SIDE
    pack = 2 * SIDE + 2 * (cells // SIDE)
    shape = pltpu.VMEM

    def kernel(*refs):
        ins, rest = refs[:15], list(refs[15:])
        l1, l2, r1, r2 = rest[4:8]
        block_kernel(cap, *ins, *rest[:4], (l1, l2), (r1, r2), *rest[8:])

    return pl.pallas_call(
        kernel,
        out_shape=jax.ShapeDtypeStruct((chans // 2, 2 * cells), BF),
        in_specs=[VMEM, VMEM, VMEM, SMEM, VMEM, VMEM, VMEM, VMEM],
        out_specs=VMEM,
        scratch_shapes=[
            shape((2 * fetched.shape[0], LANES), F32), shape((entries, 128, LANES), F32),
            shape((4 * SIDE, pack), BF), shape((entries * cells,), jnp.int32),
            pltpu.SMEM((entries * cells,), jnp.int32), shape((9, hid, chans), BF),
            shape((rows + 16, chans), F32), shape((rows + 16, hid), F32),
            shape((SIDE + 16, hid), F32), shape((SIDE + 16, hid), F32),
            shape((rows, chans), F32), shape((rows, hid), F32),
            shape((rows, chans), F32), shape((rows, hid), F32),
            shape((3, rows, hid), BF),
            shape((pack, chans), BF), shape((pack, hid), BF),
            shape((4, SIDE, chans), BF), shape((4, SIDE, hid), BF),
            shape((2, 4, SIDE, chans), BF), shape((2, 4, SIDE, hid), BF),
            shape((SIDE, chans), BF), shape((SIDE, hid), BF),
            shape(first.shape, BF), shape(first_bias.shape, F32),
            shape((9, chans, hid), BF), shape((chans, cells), BF),
            pltpu.SemaphoreType.DMA((2, 9)), pltpu.SemaphoreType.DMA((2, 9)), pltpu.SemaphoreType.DMA((7,)),
        ],
        compiler_params=pltpu.CompilerParams(
            collective_id=0, has_side_effects=True, vmem_limit_bytes=48 * 2**20
        ),
        name="conv_block",
    )(slots, counts, fetched, seam, first, first_bias, second, second_bias)


def shards(source, request_rows, cell_slots, cell_counts, seam, conv_first, bias_first, conv_second, bias_second):
    core = lax.axis_index("ch")
    tiles, slots_each = request_rows.shape[1], request_rows.shape[2]
    share = slots_each // 2
    quarter = share // 2
    cells_half = cell_slots.shape[2] // 2

    requests = lax.dynamic_slice_in_dim(request_rows[0], core * share, share, 1)
    fetched = fetch_rows(source, requests[:, None, :]).reshape(2 * tiles * quarter, LANES)

    counts = lax.dynamic_slice_in_dim(cell_counts[0], core * cells_half, cells_half, 1)
    def taps(weights):
        return weights.reshape(9, weights.shape[2], weights.shape[3])

    return conv_block(
        slots_each, cell_slots[0], counts.astype(F32).T, fetched, seam,
        taps(conv_first), bias_first[None], taps(conv_second), bias_second[None],
    )[None]


def solution(mesh):
    in_specs = (
        P("ch", ("grp", "tile")),
        P("tile", None, None),
        P("tile", None, None),
        P("tile", None, None),
        P(),
        P(None, None, "ch", None),
        P("ch"),
        P(),
        P(),
    )
    out_specs = P(("grp", "tile"), "ch", None)
    return jax.shard_map(shards, mesh=mesh, in_specs=in_specs, out_specs=out_specs, check_vma=False)
```
